256 devices in a mesh: seq: 32 (over x, y, core), dp: 8 (over z).
Axes of the slice: x: 4, y: 4, z: 8, core: 2. Of those that a mesh axis runs over, the one named last changes fastest.
Arguments:
- hidden_states: bfloat16 [8, 4096, 8192], P('dp', 'seq'), may hold values from -6 to 6
- teacher_queries: bfloat16 [8, 4096, 4096], P('dp', 'seq'), may hold values from -200 to 200
- teacher_keys: bfloat16 [8, 4096, 1024], P('dp', 'seq'), may hold values from -6 to 6
- teacher_values: bfloat16 [8, 4096, 1024], P('dp', 'seq'), may hold values from -6 to 6
- doc_ids: int32 [8, 4096], P('dp', 'seq'), may hold values from 0 to 3, never falling along the last dimension, each value on 1 to 2048 neighbouring positions
- w_proj: bfloat16 [8192, 288], P('dp'), may hold values from -0.0625 to 0.0625
- conv_weight: float32 [4, 256], replicated, may hold values from -3 to 3
- dt_bias: float32 [32], replicated, may hold values from -4 to -2
- decay_rate: float32 [32], replicated, may hold values from 0.0001 to 1
Outputs:
- grad_proj: float32 [8192, 288], P('dp')
The draws below stay inside these ranges and needn't reach their ends.
All inputs are finite; a program needn't handle non-finite values.
Results may differ from the reference program's by a relative error of at most 0.002.
The reference program's roundings to bfloat16 on the way count: a program that leaves them out, or rounds other values in their place, can miss the bound.
Values may be sent and summed in bfloat16 or wider, within the bound.
No kernel may reach another device: no remote copies, remote signals or barrier semaphores. Data moves between devices by JAX's collectives and lax.ppermute only.
A program may use at most 128 MiB of HBM per device.

```python
import math
import jax
import jax.numpy as jnp
import numpy as np
from jax import lax

D = 8192
HEADS = 32
KV_HEADS = 8
HEAD_DIM = 128
STATE = 16
CONV = 4
DOCS = 4
PROJ = 288
SEQ_LEN = 4096
SEQS = 8


def shared_keys(key):
    return jax.random.normal(key, (SEQS, SEQ_LEN, KV_HEADS * HEAD_DIM), jnp.float32)


def draw_teacher_keys(key, part):
    base = shared_keys(key)
    return jnp.clip(base, -6.0, 6.0).astype(jnp.bfloat16)


def draw_teacher_queries(key, part):
    key = jax.random.fold_in(key, 12)
    key_noise = jax.random.fold_in(key, 0)
    shape = (SEQS, SEQ_LEN, HEADS * HEAD_DIM)
    queries = 3.0 * jax.random.normal(key_noise, shape, jnp.float32)
    return jnp.clip(queries, -200.0, 200.0).astype(jnp.bfloat16)


def block_levels(own_key, shape, cuts, low, high):
    gain, own = 1.0, jax.random.fold_in(own_key, 6)
    for dim, parts in cuts:
        heights = jnp.exp(jax.random.uniform(jax.random.fold_in(own, dim), (parts,), jnp.float32, low / len(cuts), high / len(cuts)))
        gain = gain * jnp.repeat(heights, shape[dim] // parts).reshape([-1 if axis == dim else 1 for axis in range(len(shape))])
    return gain


def profile(count, total, bound, slope):
    weights = [(1 << 20) // math.isqrt(rank ** slope) + 1 for rank in range(2, count + 1)]
    surplus, given = total - bound - (count - 1), [1] * (count - 1)
    while surplus > 0:
        candidates = [i for i in range(count - 1) if given[i] < bound]
        mass, left = sum([weights[i] for i in candidates]), surplus
        for i in candidates:
            extra = min(bound - given[i], max(1, left * weights[i] // mass), surplus)
            given[i] = given[i] + extra
            surplus = surplus - extra
    return np.array([bound] + given)


def ragged_sizes(rng, amount, total, most, slope):
    if amount == 2:
        one = jax.random.randint(rng, (), max(1, total - most), min(most, total - 1) + 1)
        return jnp.stack([one, total - one])
    tallies = jnp.asarray(profile(amount, total, most, slope), jnp.int32)
    couples = (amount - 1) // 2
    donor, receiver = tallies[1:1 + 2 * couples:2], tallies[2:2 + 2 * couples:2]
    margin = jnp.minimum(donor - 1, most - receiver)
    passed = jax.random.randint(jax.random.fold_in(rng, 1), (couples,), 0, 1 << 20) % (margin + 1)
    tallies = tallies.at[1:1 + 2 * couples:2].set(donor - passed).at[2:2 + 2 * couples:2].set(receiver + passed)
    return tallies[jax.random.permutation(jax.random.fold_in(rng, 2), amount)]


def gaussian(own_key, dims, deviation, reach, cuts=(), kind=jnp.bfloat16):
    drawn = jax.random.normal(own_key, dims, jnp.float32) * deviation
    if len(cuts) > 0:
        drawn = block_levels(own_key, dims, cuts, -0.22, 0.18) * drawn
    return jnp.clip(drawn, min=-reach, max=reach).astype(kind)


def setup_inputs(seed: int = 0) -> dict:
    splits = jax.random.split(jax.random.key(seed), 10)
    hidden_states = gaussian(splits[0], (SEQS, SEQ_LEN, D), 1.0, 6.0, ((0, 8), (1, 32)))
    teacher_queries = draw_teacher_queries(jax.random.fold_in(splits[9], 71), 0)
    teacher_keys = draw_teacher_keys(jax.random.fold_in(splits[9], 71), 0)
    teacher_values = gaussian(splits[3], (SEQS, SEQ_LEN, KV_HEADS * HEAD_DIM), 1.0, 6.0, ((0, 8), (1, 32)))
    doc_ids = jax.vmap(lambda own: jnp.searchsorted(jnp.cumsum(ragged_sizes(own, DOCS, SEQ_LEN, SEQ_LEN // 2, 0)), jnp.arange(SEQ_LEN), side="right"))(jax.random.split(splits[4], SEQS)).reshape((SEQS, SEQ_LEN)).astype(jnp.int32)
    w_proj = gaussian(splits[5], (D, PROJ), D ** -0.5, 0.0625, ((0, 8),))
    conv_weight = gaussian(splits[6], (CONV, 2 * KV_HEADS * STATE), 0.5, 3.0, (), jnp.float32)
    dt_bias = jnp.clip(jax.random.uniform(splits[7], (HEADS,), jnp.float32, -4.0, -2.0), -4.0, -2.0)
    decay_rate = jnp.clip(jnp.exp(jax.random.uniform(splits[8], (HEADS,), jnp.float32, math.log(0.0001), math.log(1.0))), 0.0001, 1.0)
    return dict(hidden_states=hidden_states, teacher_queries=teacher_queries, teacher_keys=teacher_keys, teacher_values=teacher_values, doc_ids=doc_ids, w_proj=w_proj, conv_weight=conv_weight, dt_bias=dt_bias, decay_rate=decay_rate)


HIGHEST_MODE = lax.Precision.HIGHEST

def teacher_head(operands):
    query_rows, key_rows, value_rows, label_row = operands
    seq_len = query_rows.shape[0]
    scores = jnp.dot(query_rows, key_rows.T, preferred_element_type=jnp.float32) * query_rows.shape[1] ** (-0.5)
    positions = jnp.arange(seq_len)
    allowed = (positions[None, :] <= positions[:, None]) & (label_row[None, :] == label_row[:, None])
    scores = jnp.where(allowed, scores, -1e+30)
    row_max = lax.optimization_barrier(jnp.max(scores, axis=1, keepdims=True))
    weights = jnp.exp(scores - row_max)
    totals = lax.optimization_barrier(jnp.sum(weights, axis=1, keepdims=True))
    mixed_rows = jnp.dot(weights.astype(jnp.bfloat16), value_rows, preferred_element_type=jnp.float32) / totals
    return mixed_rows.astype(jnp.bfloat16)

def conv_branch(projected, labels, conv_weight):
    bc_width = conv_weight.shape[1]
    seq_len = projected.shape[0]
    source = projected[:, :bc_width]
    pre_act = conv_weight[0] * source
    for offset in range(1, conv_weight.shape[0]):
        lagged = jnp.concatenate([jnp.zeros((offset, bc_width), source.dtype), source[:seq_len - offset]], 0)
        lag_labels = jnp.concatenate([jnp.full((offset,), -1, labels.dtype), labels[:seq_len - offset]], 0)
        pre_act = pre_act + conv_weight[offset] * jnp.where((lag_labels == labels)[:, None], lagged, 0.0)
    return jax.nn.silu(pre_act)

def student_sequence(projected, value_rows, labels, conv_weight, dt_bias, decay_rate):
    seq_len = projected.shape[0]
    group_size = HEADS // KV_HEADS
    gate_width = KV_HEADS * STATE
    gates = conv_branch(projected, labels, conv_weight)
    input_gate = gates[:, :gate_width].reshape(seq_len, KV_HEADS, STATE)
    output_gate = gates[:, gate_width:].reshape(seq_len, KV_HEADS, STATE)
    step_size = jax.nn.softplus(projected[:, 2 * gate_width:] + dt_bias)
    span = min(256, seq_len)
    count_blocks = seq_len // span

    def step_block(carry, pieces):
        state_in, prev_label = carry
        b_blk, c_blk, step_blk, labels_blk, values_blk = pieces
        cum_log = jnp.cumsum(-step_blk * decay_rate, axis=0)
        order = jnp.arange(span)
        same_doc = ((labels_blk[:, None] == labels_blk[None, :]) & (order[None, :] <= order[:, None])).astype(cum_log.dtype)
        gaps = cum_log.T[:, :, None] - cum_log.T[:, None, :]
        mixing = jnp.exp(gaps * same_doc[None]) * same_doc[None] * step_blk.T[:, None, :]
        intersection = jnp.einsum('tgn,sgn->gts', c_blk, b_blk, precision=HIGHEST_MODE)
        mixing = mixing.reshape(KV_HEADS, group_size, span, span) * intersection[:, None]
        local_out = jnp.einsum('gkts,sgp->tgkp', mixing, values_blk, precision=HIGHEST_MODE)
        keep_in = (labels_blk == prev_label).astype(cum_log.dtype)
        carried = jnp.einsum('tgn,gknp->tgkp', c_blk, state_in.reshape(KV_HEADS, group_size, STATE, HEAD_DIM), precision=HIGHEST_MODE)
        scale_in = (jnp.exp(cum_log) * keep_in[:, None]).reshape(span, KV_HEADS, group_size)
        block_out = (local_out + carried * scale_in[..., None]).reshape(span, HEADS, HEAD_DIM)
        tail_same = (labels_blk == labels_blk[-1]).astype(cum_log.dtype)
        tail_weight = jnp.exp((cum_log[-1][None, :] - cum_log) * tail_same[:, None]) * tail_same[:, None] * step_blk
        state_local = jnp.einsum('sgk,sgn,sgp->gknp', tail_weight.reshape(span, KV_HEADS, group_size), b_blk, values_blk, precision=HIGHEST_MODE)
        state_local = state_local.reshape(HEADS, STATE, HEAD_DIM)
        decay_total = jnp.exp(cum_log[-1]) * keep_in[-1]
        new_state = decay_total[:, None, None] * state_in + state_local
        return ((new_state, labels_blk[-1]), block_out)
    pieces = (input_gate.reshape(count_blocks, span, KV_HEADS, STATE), output_gate.reshape(count_blocks, span, KV_HEADS, STATE), step_size.reshape(count_blocks, span, HEADS), labels.reshape(count_blocks, span), value_rows.reshape(count_blocks, span, KV_HEADS, HEAD_DIM))
    initial = (jnp.zeros((HEADS, STATE, HEAD_DIM), projected.dtype), jnp.array(-1, jnp.int32))
    _, outputs = lax.scan(jax.checkpoint(step_block), initial, pieces)
    return outputs.reshape(seq_len, HEADS, HEAD_DIM)

def reference(hidden_states, teacher_queries, teacher_keys, teacher_values, doc_ids, w_proj, conv_weight, dt_bias, decay_rate):
    group_size = HEADS // KV_HEADS
    loss_weight = 1.0 / math.sqrt(HEADS * HEAD_DIM * SEQS * SEQ_LEN)

    def one_sequence(operands):
        tokens_in, queries, key_rows, values, labels = operands
        query_heads = queries.reshape(SEQ_LEN, HEADS, HEAD_DIM).transpose(1, 0, 2)
        key_heads = jnp.repeat(key_rows.reshape(SEQ_LEN, KV_HEADS, HEAD_DIM).transpose(1, 0, 2), group_size, axis=0)
        value_heads = jnp.repeat(values.reshape(SEQ_LEN, KV_HEADS, HEAD_DIM).transpose(1, 0, 2), group_size, axis=0)
        label_rows = jnp.broadcast_to(labels, (HEADS, SEQ_LEN))
        teacher = lax.map(teacher_head, (query_heads, key_heads, value_heads, label_rows))
        teacher = teacher.transpose(1, 0, 2).astype(jnp.float32)
        projected = jnp.dot(tokens_in, w_proj, preferred_element_type=jnp.float32)
        value_rows = values.reshape(SEQ_LEN, KV_HEADS, HEAD_DIM).astype(jnp.float32)

        def run_student(proj_rows):
            return student_sequence(proj_rows, value_rows, labels, conv_weight, dt_bias, decay_rate)
        student_out, pull_back = jax.vjp(run_student, projected)
        grad_pre = pull_back((student_out - teacher) * loss_weight)[0]
        return jnp.dot(tokens_in.T, grad_pre.astype(jnp.bfloat16), preferred_element_type=jnp.float32)
    seq_grads = lax.map(one_sequence, (hidden_states, teacher_queries, teacher_keys, teacher_values, doc_ids))
    return lax.optimization_barrier(jnp.sum(seq_grads, axis=0))
```

```python
import math

import jax
import jax.numpy as jnp
from jax import lax
from jax.experimental import pallas as pl
from jax.experimental.pallas import tpu as pltpu
from jax.sharding import PartitionSpec as P

D = 8192
HEADS = 32
GROUPS = 8
SHARE = 4
DIM = 128
STATE = 16
TAPS = 4
SEQ = 4096
ROWS = 128
BLOCKS = SEQ // ROWS
PARTS = 8
DOC_ROWS = 16
TEACH_ROWS = 2 * ROWS + DOC_ROWS
COLS = 40
SPAN = 256
CHUNKS = SEQ // SPAN
KEYS = 512
PAD = 256
GRAD_ROWS = 48
QUARTER = SEQ // SHARE

F32 = jnp.float32
BF16 = jnp.bfloat16
NEG = -1e30
VMEM = pl.BlockSpec(memory_space=pltpu.VMEM)
SMEM = pl.BlockSpec(memory_space=pltpu.SMEM)

NT = (((1,), (1,)), ((), ()))


def params(mib=56):
    return pltpu.CompilerParams(vmem_limit_bytes=mib << 20)


def mm(a, b):
    return jnp.dot(a, b, preferred_element_type=F32)


def mm_nt(a, b):
    return lax.dot_general(a, b, NT, preferred_element_type=F32)


def split(x):
    high = x.astype(BF16)
    return high, (x - high.astype(F32)).astype(BF16)


def doc_start(position, n_ref):
    start = jnp.where(position >= n_ref[0], n_ref[0], 0)
    start = jnp.where(position >= n_ref[1], n_ref[1], start)
    return jnp.where(position >= n_ref[2], n_ref[2], start)


def scalar_start(position, n_ref):
    return doc_start(position, n_ref)


def pack_teacher_kernel(q_ref, k_ref, v_ref, doc_ref, out_ref):
    docs = jnp.broadcast_to(doc_ref[...].astype(F32), (DOC_ROWS, ROWS)).astype(BF16)
    for h in range(HEADS):
        g = h // SHARE
        out_ref[h, 0:ROWS, :] = q_ref[0, :, h * DIM : (h + 1) * DIM]
        source = k_ref if h % 2 == 0 else v_ref
        out_ref[h, ROWS : 2 * ROWS, :] = source[0, :, g * DIM : (g + 1) * DIM]
        out_ref[h, 2 * ROWS :, :] = docs


def pack_teacher(q, k, v, docs):
    return pl.pallas_call(
        pack_teacher_kernel,
        out_shape=jax.ShapeDtypeStruct((HEADS, TEACH_ROWS, DIM), BF16),
        in_specs=[VMEM] * 4,
        out_specs=VMEM,
        compiler_params=params(32),
        cost_estimate=pl.CostEstimate(flops=0, bytes_accessed=4 << 20, transcendentals=0),
    )(q, k, v, docs)


def pack_hidden_kernel(hid_ref, out_ref):
    for g in range(GROUPS):
        for d in range(PARTS):
            at = d * 1024 + g * 128
            out_ref[g, :, d * 128 : (d + 1) * 128] = hid_ref[0, :, at : at + 128]


def pack_hidden(hidden):
    return pl.pallas_call(
        pack_hidden_kernel,
        out_shape=jax.ShapeDtypeStruct((GROUPS, ROWS, D // GROUPS), BF16),
        in_specs=[VMEM],
        out_specs=VMEM,
        compiler_params=params(32),
        cost_estimate=pl.CostEstimate(flops=0, bytes_accessed=4 << 20, transcendentals=0),
    )(hidden)


def project_kernel(core_ref, hid_ref, own_ref, other_ref, out_ref, acc_ref):
    step = pl.program_id(0)
    half = own_ref.shape[1]
    mine = pl.multiple_of(core_ref[0] * half, half)
    theirs = pl.multiple_of((1 - core_ref[0]) * half, half)
    part = mm(hid_ref[0, :, pl.ds(mine, half)], own_ref[0])
    part = part + mm(hid_ref[0, :, pl.ds(theirs, half)], other_ref[0])

    @pl.when(step == 0)
    def _():
        acc_ref[...] = jnp.zeros_like(acc_ref)

    acc_ref[:, : part.shape[1]] += part

    @pl.when(step == PARTS - 1)
    def _():
        turned = acc_ref[...].T
        for h in range(HEADS):
            g = h // SHARE
            out_ref[h, 0:STATE, :] = turned[g * STATE : (g + 1) * STATE]
            out_ref[h, STATE : 2 * STATE, :] = turned[128 + g * STATE : 128 + (g + 1) * STATE]
            out_ref[h, 2 * STATE :, :] = jnp.broadcast_to(
                turned[256 + h : 257 + h], (COLS - 2 * STATE, ROWS)
            )


def project(core, hidden, own, other):
    width = own.shape[2]
    half = own.shape[1]
    return pl.pallas_call(
        project_kernel,
        out_shape=jax.ShapeDtypeStruct((HEADS, COLS, ROWS), F32),
        grid_spec=pltpu.PrefetchScalarGridSpec(
            num_scalar_prefetch=1,
            grid=(PARTS,),
            in_specs=[
                pl.BlockSpec((1, ROWS, 2 * half), lambda i, c: (0, 0, i)),
                pl.BlockSpec((1, half, width), lambda i, c: (i, 0, 0)),
                pl.BlockSpec((1, half, width), lambda i, c: (i, 0, 0)),
            ],
            out_specs=pl.BlockSpec((HEADS, COLS, ROWS), lambda i, c: (0, 0, 0)),
            scratch_shapes=[pltpu.VMEM((ROWS, 384), F32)],
        ),
        compiler_params=params(32),
        cost_estimate=pl.CostEstimate(
            flops=2 * ROWS * D * 288, bytes_accessed=8 << 20, transcendentals=0
        ),
    )(core, hidden, own, other)


def attend_kernel(
    core_ref, own_ref, other_ref, teach_ref, v_ref, vt_ref, n_ref, keys, turned, scores
):
    docs = jnp.max(own_ref[:, 2 * ROWS :, :].astype(F32), axis=1)
    for d in range(3):
        n_ref[d] = jnp.sum((docs < d + 0.5).astype(F32)).astype(jnp.int32)
    n_ref[3] = 0
    keys[0:PAD, :] = jnp.zeros((PAD, DIM), BF16)
    turned[:, 0:PAD] = jnp.zeros((DIM, PAD), BF16)

    @pl.when(core_ref[0] == 0)
    def _():
        for s in range(BLOCKS):
            keys[PAD + s * ROWS : PAD + (s + 1) * ROWS, :] = own_ref[s, ROWS : 2 * ROWS, :]
            v_ref[s * ROWS : (s + 1) * ROWS, :] = other_ref[s]

    @pl.when(core_ref[0] != 0)
    def _():
        for s in range(BLOCKS):
            keys[PAD + s * ROWS : PAD + (s + 1) * ROWS, :] = other_ref[s]
            v_ref[s * ROWS : (s + 1) * ROWS, :] = own_ref[s, ROWS : 2 * ROWS, :]

    for s in range(BLOCKS):
        block = v_ref[s * ROWS : (s + 1) * ROWS, :].astype(F32).T.astype(BF16)
        turned[:, PAD + s * ROWS : PAD + (s + 1) * ROWS] = block
        vt_ref[:, s * ROWS : (s + 1) * ROWS] = block

    scale = DIM ** (-0.5) * math.log2(math.e)

    def rows(i, carry):
        q0 = i * SPAN
        query = jnp.concatenate([own_ref[2 * i, 0:ROWS, :], own_ref[2 * i + 1, 0:ROWS, :]], 0)
        first = scalar_start(q0, n_ref)
        last = scalar_start(q0 + SPAN - 1, n_ref)
        count = (q0 + SPAN - first + KEYS - 1) // KEYS
        q_at = q0 + lax.broadcasted_iota(jnp.int32, (1, SPAN), 1)
        start = doc_start(q_at, n_ref)

        def score(j, top):
            low = q0 + SPAN - (j + 1) * KEYS
            at = pl.multiple_of(low + PAD, SPAN)
            s = mm_nt(keys[pl.ds(at, KEYS), :], query)
            k_at = low + lax.broadcasted_iota(jnp.int32, (KEYS, SPAN), 0)
            s = jnp.where((k_at <= q_at) & (k_at >= start), s, NEG)
            scores[pl.ds(pl.multiple_of(j * KEYS, KEYS), KEYS), :] = s
            return jnp.maximum(top, jnp.max(s.reshape(KEYS // 8, 8, SPAN), axis=0))

        def score_plain(j, top):
            low = q0 + SPAN - (j + 1) * KEYS
            at = pl.multiple_of(low + PAD, SPAN)
            s = mm_nt(keys[pl.ds(at, KEYS), :], query)
            scores[pl.ds(pl.multiple_of(j * KEYS, KEYS), KEYS), :] = s
            return jnp.maximum(top, jnp.max(s.reshape(KEYS // 8, 8, SPAN), axis=0))

        top = score(0, jnp.full((8, SPAN), NEG, F32))
        inner = jnp.clip((q0 + SPAN - last) // KEYS, 1, count)
        top = lax.fori_loop(1, inner, score_plain, top)
        top = lax.fori_loop(inner, count, score, top)
        top = jnp.max(top, axis=0, keepdims=True)

        def mix(j, state):
            total, out = state
            low = q0 + SPAN - (j + 1) * KEYS
            at = pl.multiple_of(low + PAD, SPAN)
            s = scores[pl.ds(pl.multiple_of(j * KEYS, KEYS), KEYS), :]
            p = jnp.exp2((s - top) * scale)
            total = total + jnp.sum(p.reshape(KEYS // 8, 8, SPAN), axis=0)
            out = out + mm(turned[:, pl.ds(at, KEYS)], p.astype(BF16))
            return total, out

        total, out = lax.fori_loop(
            0, count, mix, (jnp.zeros((8, SPAN), F32), jnp.zeros((DIM, SPAN), F32))
        )
        total = jnp.sum(total, axis=0, keepdims=True)
        teach_ref[:, pl.ds(pl.multiple_of(q0, SPAN), SPAN)] = (out / total).astype(BF16)
        return carry

    lax.fori_loop(0, CHUNKS, rows, 0)


def attend(core, own, other):
    return pl.pallas_call(
        attend_kernel,
        out_shape=(
            jax.ShapeDtypeStruct((DIM, SEQ), BF16),
            jax.ShapeDtypeStruct((SEQ, DIM), BF16),
            jax.ShapeDtypeStruct((DIM, SEQ), BF16),
            jax.ShapeDtypeStruct((4,), jnp.int32),
        ),
        in_specs=[SMEM, VMEM, VMEM],
        out_specs=(VMEM, VMEM, VMEM, SMEM),
        scratch_shapes=[
            pltpu.VMEM((PAD + SEQ, DIM), BF16),
            pltpu.VMEM((DIM, PAD + SEQ), BF16),
            pltpu.VMEM((SEQ + KEYS, SPAN), F32),
        ],
        compiler_params=params(),
        cost_estimate=pl.CostEstimate(
            flops=8 << 30, bytes_accessed=8 << 20, transcendentals=8 << 20
        ),
    )(core, own, other)


def scan_lanes(x, reverse):
    width = x.shape[1]
    lane = lax.broadcasted_iota(jnp.int32, x.shape, 1)
    step = 1
    while step < width:
        if reverse:
            moved = pltpu.roll(x, width - step, 1)
            x = x + jnp.where(lane < width - step, moved, 0.0)
        else:
            moved = pltpu.roll(x, step, 1)
            x = x + jnp.where(lane >= step, moved, 0.0)
        step *= 2
    return x


def student_kernel(
    head_ref,
    n_ref,
    bias_ref,
    rate_ref,
    taps_ref,
    proj_ref,
    teach_ref,
    v_ref,
    vt_ref,
    out_ref,
    source,
    steps,
    cums,
    columns,
    pre_s,
    sig_s,
    z_s,
    dc_s,
    q_s,
    x_s,
    direct_s,
    state_s,
    dstate_s,
    *,
    weight,
):
    head = head_ref[0]
    group = head // SHARE
    bias = bias_ref[head]
    rate = rate_ref[head]
    lane = lax.broadcasted_iota(jnp.int32, (1, SPAN), 1)
    deep = lax.broadcasted_iota(jnp.int32, (SPAN, SPAN), 0)
    taps_b = taps_ref[pl.ds(pl.multiple_of(group * STATE, STATE), STATE), :]
    taps_c = taps_ref[pl.ds(pl.multiple_of(128 + group * STATE, STATE), STATE), :]
    taps = jnp.concatenate([taps_b, taps_c], 0)

    source[:, 0:128] = jnp.zeros((2 * STATE, 128), F32)
    for s in range(BLOCKS):
        source[:, 128 + s * ROWS : 128 + (s + 1) * ROWS] = proj_ref[s, 0 : 2 * STATE, :]
        steps[s // 2 : s // 2 + 1, (s % 2) * ROWS : (s % 2 + 1) * ROWS] = proj_ref[
            s, 2 * STATE : 2 * STATE + 1, :
        ]
    raw = steps[...] + bias
    step_all = jnp.maximum(raw, 0.0) + jnp.log1p(jnp.exp(-jnp.abs(raw)))
    slope_all = 1.0 / (1.0 + jnp.exp(-raw))
    steps[...] = step_all
    cum_all = scan_lanes(-step_all * rate, False)
    cums[...] = cum_all
    cum_turned = cum_all.T
    for c in range(CHUNKS):
        columns[c] = cum_turned[:, c : c + 1]

    def marks(c):
        base = c * SPAN
        at = base + lane
        start = doc_start(at, n_ref)
        last = scalar_start(base + SPAN - 1, n_ref)
        return base, at, start, last

    def forward(c, state):
        base, at, start, last = marks(c)
        wide = pl.multiple_of(base, SPAN)
        rows = source[:, pl.ds(wide, SPAN + 128)]
        pre = taps[:, 0:1] * rows[:, 128:]
        for j in range(1, TAPS):
            lagged = jnp.where(at - j >= start, pltpu.roll(rows, j, 1)[:, 128:], 0.0)
            pre = pre + taps[:, j : j + 1] * lagged
        sig = 1.0 / (1.0 + jnp.exp(-pre))
        gates = pre * sig
        pre_s[:, pl.ds(wide, SPAN)] = pre
        sig_s[:, pl.ds(wide, SPAN)] = sig
        gate_c = gates[STATE:]
        step = steps[pl.ds(c, 1), :]
        cum = cums[pl.ds(c, 1), :]
        ended = cum[:, SPAN - 1 :]
        fed = gates[:STATE] * step
        fed_high, fed_low = split(fed)
        c_high, c_low = split(gate_c)
        fed_stack = jnp.concatenate([fed, fed_low.astype(F32), fed], 0)
        left = fed_stack.T.astype(BF16)
        inner = mm(left, jnp.concatenate([c_high, c_high, c_low], 0))
        allowed = (deep <= lane) & (deep >= start - base)
        fade = jnp.exp(jnp.where(allowed, cum - columns[c], NEG))
        mixing = fade * inner
        mix_high, mix_low = split(mixing)
        values = v_ref[pl.ds(wide, SPAN), :]
        turned = vt_ref[:, pl.ds(wide, SPAN)]
        enter = jnp.where(start < base, jnp.exp(cum), 0.0)
        entered = gate_c * enter
        in_high, in_low = split(entered)
        s_high, s_low = split(state)
        state_left = jnp.concatenate([state, s_low.astype(F32), state], 0).T.astype(BF16)
        out = mm(turned, mix_high) + mm(turned, mix_low)
        out = out + mm(state_left, jnp.concatenate([in_high, in_high, in_low], 0))
        wanted = teach_ref[:, pl.ds(wide, SPAN)].astype(F32)
        error = (out - wanted) * weight
        q_s[pl.ds(c, 1), :] = jnp.sum(out * error, axis=0, keepdims=True)
        e_high, e_low = split(error)
        e_stack = jnp.concatenate([e_high, e_low], 0)
        pulled = fade * mm(jnp.concatenate([values, values], 1), e_stack)
        h_high, h_low = split(pulled)
        c_stack = jnp.concatenate([c_high, c_low], 0)
        z = mm_nt(c_stack, h_high) + mm_nt(c_stack, h_low)
        z_s[:, pl.ds(wide, SPAN)] = z[:STATE] + z[STATE:]
        fed_pair = jnp.concatenate([fed_high, fed_low], 0)
        dc = mm(fed_pair, h_high) + mm(fed_pair, h_low)
        s_pair = jnp.concatenate([s_high, s_low], 0)
        dc_in = mm(s_pair, e_high) + mm(s_pair, e_low)
        dc_s[:, pl.ds(wide, SPAN)] = dc[:STATE] + dc[STATE:] + enter * (dc_in[:STATE] + dc_in[STATE:])
        in_pair = jnp.concatenate([in_high, in_low], 0)
        ds = mm_nt(in_pair, e_high) + mm_nt(in_pair, e_low)
        dstate_s[c] = ds[:STATE] + ds[STATE:]
        state_s[c] = state
        tail = jnp.where(at >= last, jnp.exp(ended - cum), 0.0)
        t_high, t_low = split(fed * tail)
        new = mm(jnp.concatenate([t_high, t_low], 0), values)
        keep = jnp.where(last < base, 1.0, 0.0) * jnp.exp(ended)
        return keep * state + new[:STATE] + new[STATE:]

    final = lax.fori_loop(0, CHUNKS, forward, jnp.zeros((STATE, DIM), F32))
    state_s[CHUNKS] = final

    def backward(k, carried):
        dstate, later = carried
        c = CHUNKS - 1 - k
        base, at, start, last = marks(c)
        wide = pl.multiple_of(base, SPAN)
        step = steps[pl.ds(c, 1), :]
        cum = cums[pl.ds(c, 1), :]
        ended = cum[:, SPAN - 1 :]
        tail = jnp.where(at >= last, jnp.exp(ended - cum), 0.0)
        d_high, d_low = split(dstate)
        turned = vt_ref[:, pl.ds(wide, SPAN)]
        through = mm(jnp.concatenate([d_high, d_low], 0), turned)
        z = z_s[:, pl.ds(wide, SPAN)] + tail * (through[:STATE] + through[STATE:])
        pre = pre_s[:, pl.ds(wide, SPAN)]
        sig = sig_s[:, pl.ds(wide, SPAN)]
        gates = pre * sig
        direct = jnp.sum(gates[:STATE] * z, axis=0, keepdims=True)
        direct_s[pl.ds(c, 1), :] = direct
        crossing = jnp.sum(jnp.sum(dstate * state_s[c + 1], axis=0, keepdims=True), axis=1, keepdims=True)
        x_s[pl.ds(c, 1), :] = jnp.broadcast_to(crossing, (1, SPAN))
        dgates = jnp.concatenate([step * z, dc_s[:, pl.ds(wide, SPAN)]], 0)
        dpre = dgates * (sig + gates * (1.0 - sig))
        rows = jnp.concatenate([dpre, later], 1)
        back = taps[:, 0:1] * rows[:, :SPAN]
        for j in range(1, TAPS):
            reach = jnp.where(at >= doc_start(at + j, n_ref), pltpu.roll(rows, SPAN + 128 - j, 1)[:, :SPAN], 0.0)
            back = back + taps[:, j : j + 1] * reach
        column = pl.multiple_of((c // 2) * ROWS, ROWS)
        out_ref[2 * (c % 2), 0 : 2 * STATE, pl.ds(column, ROWS)] = back[:, :ROWS]
        out_ref[2 * (c % 2) + 1, 0 : 2 * STATE, pl.ds(column, ROWS)] = back[:, ROWS:]
        keep = jnp.where(last < base, 1.0, 0.0) * jnp.exp(ended)
        return keep * dstate + dstate_s[c], dpre[:, :128]

    nothing = (jnp.zeros((STATE, DIM), F32), jnp.zeros((2 * STATE, 128), F32))
    lax.fori_loop(0, CHUNKS, backward, nothing)

    at_all = lax.broadcasted_iota(jnp.int32, (CHUNKS, SPAN), 0) * SPAN
    at_all = at_all + lax.broadcasted_iota(jnp.int32, (CHUNKS, SPAN), 1)
    direct = direct_s[...]
    dlog = scan_lanes(q_s[...] - step_all * direct, True) + x_s[...]
    dlog = jnp.where(at_all > doc_start(at_all, n_ref), dlog, 0.0)
    dstep = (direct - rate * dlog) * slope_all
    for s in range(BLOCKS):
        piece = dstep[s // 2 : s // 2 + 1, (s % 2) * ROWS : (s % 2 + 1) * ROWS]
        out_ref[s % SHARE, 2 * STATE :, (s // SHARE) * ROWS : (s // SHARE + 1) * ROWS] = (
            jnp.broadcast_to(piece, (COLS - 2 * STATE, ROWS))
        )


def student(head, counts, bias, rate, taps, proj, teach, v, vt, weight):
    return pl.pallas_call(
        lambda *refs: student_kernel(*refs, weight=weight),
        out_shape=jax.ShapeDtypeStruct((SHARE, COLS, QUARTER), F32),
        in_specs=[SMEM, SMEM, SMEM, SMEM, VMEM, VMEM, VMEM, VMEM, VMEM],
        out_specs=VMEM,
        scratch_shapes=[
            pltpu.VMEM((2 * STATE, 128 + SEQ), F32),
            pltpu.VMEM((CHUNKS, SPAN), F32),
            pltpu.VMEM((CHUNKS, SPAN), F32),
            pltpu.VMEM((CHUNKS, SPAN, 1), F32),
            pltpu.VMEM((2 * STATE, SEQ), F32),
            pltpu.VMEM((2 * STATE, SEQ), F32),
            pltpu.VMEM((STATE, SEQ), F32),
            pltpu.VMEM((STATE, SEQ), F32),
            pltpu.VMEM((CHUNKS, SPAN), F32),
            pltpu.VMEM((CHUNKS, SPAN), F32),
            pltpu.VMEM((CHUNKS, SPAN), F32),
            pltpu.VMEM((CHUNKS + 1, STATE, DIM), F32),
            pltpu.VMEM((CHUNKS, STATE, DIM), F32),
        ],
        compiler_params=params(),
        cost_estimate=pl.CostEstimate(
            flops=8 << 30, bytes_accessed=8 << 20, transcendentals=4 << 20
        ),
    )(head, counts, bias, rate, taps, proj, teach, v, vt)


def combine_kernel(in_ref, out_ref):
    gates = in_ref[0, : 2 * STATE] + in_ref[1, : 2 * STATE]
    gates = gates + in_ref[2, : 2 * STATE]
    gates = gates + in_ref[3, : 2 * STATE]
    steps = [in_ref[k, 2 * STATE : 2 * STATE + 1] for k in range(SHARE)]
    rest = jnp.zeros((GRAD_ROWS - 2 * STATE - SHARE, QUARTER), F32)
    rounded = jnp.concatenate([gates] + steps + [rest], 0).astype(BF16)
    for g in range(GROUPS):
        out_ref[g] = rounded


def combine(parts):
    return pl.pallas_call(
        combine_kernel,
        out_shape=jax.ShapeDtypeStruct((GROUPS, GRAD_ROWS, QUARTER), BF16),
        in_specs=[VMEM],
        out_specs=VMEM,
        compiler_params=params(32),
    )(parts)


def product_kernel(grad_ref, hid_ref, out_ref):
    for half in range(2):
        left = grad_ref[half * 4 : half * 4 + 4].reshape(4 * GRAD_ROWS, QUARTER)
        left = left.astype(F32)
        keep = jnp.concatenate(
            [left[i * GRAD_ROWS : i * GRAD_ROWS + COLS] for i in range(4)], 0
        ).astype(BF16)
        for d in range(PARTS):
            hid = hid_ref[:, :, d * 128 : (d + 1) * 128].reshape(QUARTER, 128)
            part = mm(keep, hid)
            out_ref[2 * half, d] = part[: 2 * COLS]
            out_ref[2 * half + 1, d] = part[2 * COLS :]


def product(grads, hidden):
    return pl.pallas_call(
        product_kernel,
        out_shape=jax.ShapeDtypeStruct((SHARE, PARTS, 2 * COLS, 128), F32),
        in_specs=[VMEM, VMEM],
        out_specs=VMEM,
        compiler_params=params(32),
        cost_estimate=pl.CostEstimate(
            flops=2 * 320 * 1024 * 1024, bytes_accessed=4 << 20, transcendentals=0
        ),
    )(grads, hidden)


def place_kernel(in_ref, out_ref):
    for g in range(GROUPS):
        gates_b, gates_c, steps = [], [], []
        for k in range(GROUPS):
            block = in_ref[SHARE * g + k // 2]
            at = (k % 2) * COLS
            gates_b.append(block[at : at + STATE])
            gates_c.append(block[at + STATE : at + 2 * STATE])
            steps.append(block[at + 2 * STATE : at + 2 * STATE + SHARE])
        fill = jnp.zeros((96, 128), F32)
        rows = jnp.concatenate(gates_b + gates_c + steps + [fill], 0)
        out_ref[g * 128 : (g + 1) * 128, :] = rows.T[:, :288]


def place(blocks):
    return pl.pallas_call(
        place_kernel,
        out_shape=jax.ShapeDtypeStruct((1024, 288), F32),
        in_specs=[VMEM],
        out_specs=VMEM,
        compiler_params=params(32),
    )(blocks)


def swap_all(x, axis, groups=None):
    return lax.all_to_all(x, axis, 0, 0, tiled=True, axis_index_groups=groups)


def local(hidden, queries, keys, values, docs, w_proj, conv_weight, dt_bias, decay_rate):
    seq_devices = lax.axis_size("seq")
    data_devices = lax.axis_size("dp")
    seq_len = hidden.shape[1] * seq_devices
    weight = 1.0 / math.sqrt(HEADS * DIM * data_devices * seq_len)
    head = lax.axis_index("seq").astype(jnp.int32)
    core = head % 2
    fours = [[SHARE * g + j for j in range(SHARE)] for g in range(GROUPS)]
    eights = [[SHARE * g + j for g in range(GROUPS)] for j in range(SHARE)]
    partner = [(i, i ^ 1) for i in range(seq_devices)]

    half = w_proj.shape[0] // 2
    own_w = lax.all_gather(lax.dynamic_slice_in_dim(w_proj, core * half, half, 0), "dp", axis=0)
    other_w = lax.ppermute(own_w, "seq", partner)

    own = swap_all(pack_teacher(queries, keys, values, docs), "seq")
    other = lax.ppermute(own[:, ROWS : 2 * ROWS, :], "seq", partner)
    proj = swap_all(project(core[None], hidden, own_w, other_w), "seq")
    teach, v, vt, counts = attend(core[None], own, other)
    hidden_packed = pack_hidden(hidden)
    hidden_packed, proj = lax.optimization_barrier((hidden_packed, proj))
    hidden_part = swap_all(hidden_packed, "seq", eights)
    grads = student(
        head[None], counts, dt_bias, decay_rate, conv_weight.T, proj, teach, v, vt, weight
    )
    quarter = combine(swap_all(grads, "seq", fours))
    spread = swap_all(quarter, "seq", eights)
    partial = product(spread, hidden_part)
    partial = jnp.sum(swap_all(partial, "seq", fours), axis=0)
    total = jnp.sum(swap_all(partial, "dp"), axis=0)
    blocks = swap_all(jnp.broadcast_to(total[None], (seq_devices, 2 * COLS, 128)), "seq")
    return place(blocks)


def solution(mesh):
    placed = (
        P("dp", "seq", None),
        P("dp", "seq", None),
        P("dp", "seq", None),
        P("dp", "seq", None),
        P("dp", "seq"),
        P("dp", None),
        P(),
        P(),
        P(),
    )
    return jax.shard_map(
        local, mesh=mesh, in_specs=placed, out_specs=P("dp", None), check_vma=False
    )
```

```python
import math

import jax
import jax.numpy as jnp
from jax import lax
from jax.experimental import pallas as pl
from jax.experimental.pallas import tpu as pltpu
from jax.sharding import PartitionSpec as P

D = 8192
HEADS = 32
GROUPS = 8
SHARE = 4
DIM = 128
STATE = 16
TAPS = 4
SEQ = 4096
ROWS = 128
BLOCKS = SEQ // ROWS
PARTS = 8
DOC_ROWS = 16
TEACH_ROWS = 2 * ROWS + DOC_ROWS
COLS = 40
SPAN = 256
CHUNKS = SEQ // SPAN
KEYS = 512
PAD = 256
QUARTER = SEQ // SHARE

F32 = jnp.float32
BF16 = jnp.bfloat16
NEG = -1e30
VMEM = pl.BlockSpec(memory_space=pltpu.VMEM)
SMEM = pl.BlockSpec(memory_space=pltpu.SMEM)

NT = (((1,), (1,)), ((), ()))


def params(mib=56):
    return pltpu.CompilerParams(vmem_limit_bytes=mib << 20)


def mm(a, b):
    return jnp.dot(a, b, preferred_element_type=F32)


def mm_nt(a, b):
    return lax.dot_general(a, b, NT, preferred_element_type=F32)


def split(x):
    high = x.astype(BF16)
    return high, (x - high.astype(F32)).astype(BF16)


def doc_start(position, n_ref):
    start = jnp.where(position >= n_ref[0], n_ref[0], 0)
    start = jnp.where(position >= n_ref[1], n_ref[1], start)
    return jnp.where(position >= n_ref[2], n_ref[2], start)


def scalar_start(position, n_ref):
    return doc_start(position, n_ref)


def pack_teacher_kernel(q_ref, k_ref, v_ref, doc_ref, out_ref):
    docs = jnp.broadcast_to(doc_ref[...].astype(F32), (DOC_ROWS, ROWS)).astype(BF16)
    for k in range(SHARE):
        out_ref[k, 0:ROWS, :] = q_ref[0, :, k * DIM : (k + 1) * DIM]
        source = k_ref if k % 2 == 0 else v_ref
        out_ref[k, ROWS : 2 * ROWS, :] = source[0]
        out_ref[k, 2 * ROWS :, :] = docs


def pack_teacher(q, k, v, docs):
    return pl.pallas_call(
        pack_teacher_kernel,
        out_shape=jax.ShapeDtypeStruct((HEADS, TEACH_ROWS, DIM), BF16),
        grid=(GROUPS,),
        in_specs=[
            pl.BlockSpec((1, ROWS, SHARE * DIM), lambda g: (0, 0, g)),
            pl.BlockSpec((1, ROWS, DIM), lambda g: (0, 0, g)),
            pl.BlockSpec((1, ROWS, DIM), lambda g: (0, 0, g)),
            pl.BlockSpec((1, ROWS), lambda g: (0, 0)),
        ],
        out_specs=pl.BlockSpec((SHARE, TEACH_ROWS, DIM), lambda g: (g, 0, 0)),
        compiler_params=params(60),
        cost_estimate=pl.CostEstimate(flops=0, bytes_accessed=4 << 20, transcendentals=0),
    )(q, k, v, docs)


def pack_hidden_kernel(hid_ref, out_ref):
    for g in range(GROUPS):
        for c in range(2):
            for i in range(PARTS // 2):
                at = (4 * c + i) * 1024 + g * 128
                out_ref[2 * g + c, :, i * 128 : (i + 1) * 128] = hid_ref[0, :, at : at + 128]


def pack_hidden(hidden):
    return pl.pallas_call(
        pack_hidden_kernel,
        out_shape=jax.ShapeDtypeStruct((2 * GROUPS, ROWS, D // 16), BF16),
        in_specs=[VMEM],
        out_specs=VMEM,
        compiler_params=params(60),
        cost_estimate=pl.CostEstimate(flops=0, bytes_accessed=4 << 20, transcendentals=0),
    )(hidden)


def project_kernel(core_ref, hid_ref, own_ref, other_ref, out_ref, acc_ref):
    step = pl.program_id(0)
    half = own_ref.shape[2]
    mine = pl.multiple_of(core_ref[0] * half, half)
    theirs = pl.multiple_of((1 - core_ref[0]) * half, half)

    @pl.when(step == 0)
    def _():
        acc_ref[...] = jnp.zeros_like(acc_ref)

    part = mm_nt(own_ref[0], hid_ref[0, :, pl.ds(mine, half)])
    acc_ref[...] += part + mm_nt(other_ref[0], hid_ref[0, :, pl.ds(theirs, half)])

    @pl.when(step == PARTS - 1)
    def _():
        for h in range(HEADS):
            g = h // SHARE
            out_ref[h, 0:STATE, :] = acc_ref[g * STATE : (g + 1) * STATE]
            out_ref[h, STATE : 2 * STATE, :] = acc_ref[128 + g * STATE : 128 + (g + 1) * STATE]
            out_ref[h, 2 * STATE :, :] = jnp.broadcast_to(
                acc_ref[256 + h : 257 + h], (COLS - 2 * STATE, ROWS)
            )


def project(core, hidden, own, other):
    width = own.shape[1]
    half = own.shape[2]
    return pl.pallas_call(
        project_kernel,
        out_shape=jax.ShapeDtypeStruct((HEADS, COLS, ROWS), F32),
        grid_spec=pltpu.PrefetchScalarGridSpec(
            num_scalar_prefetch=1,
            grid=(PARTS,),
            in_specs=[
                pl.BlockSpec((1, ROWS, 2 * half), lambda i, c: (0, 0, i)),
                pl.BlockSpec((1, width, half), lambda i, c: (i, 0, 0)),
                pl.BlockSpec((1, width, half), lambda i, c: (i, 0, 0)),
            ],
            out_specs=pl.BlockSpec((HEADS, COLS, ROWS), lambda i, c: (0, 0, 0)),
            scratch_shapes=[pltpu.VMEM((width, ROWS), F32)],
        ),
        compiler_params=params(60),
        cost_estimate=pl.CostEstimate(
            flops=2 * ROWS * D * 288, bytes_accessed=8 << 20, transcendentals=0
        ),
    )(core, hidden, own, other)


def attend_kernel(
    core_ref, own_ref, other_ref, teach_ref, v_ref, vt_ref, n_ref, keys, turned, scores
):
    docs = jnp.max(own_ref[:, 2 * ROWS :, :].astype(F32), axis=1)
    for d in range(3):
        n_ref[d] = jnp.sum((docs < d + 0.5).astype(F32)).astype(jnp.int32)
    n_ref[3] = 0
    keys[0:PAD, :] = jnp.zeros((PAD, DIM), BF16)
    turned[:, 0:PAD] = jnp.zeros((DIM, PAD), BF16)

    @pl.when(core_ref[0] == 0)
    def _():
        for s in range(BLOCKS):
            keys[PAD + s * ROWS : PAD + (s + 1) * ROWS, :] = own_ref[s, ROWS : 2 * ROWS, :]
            v_ref[s * ROWS : (s + 1) * ROWS, :] = other_ref[s]

    @pl.when(core_ref[0] != 0)
    def _():
        for s in range(BLOCKS):
            keys[PAD + s * ROWS : PAD + (s + 1) * ROWS, :] = other_ref[s]
            v_ref[s * ROWS : (s + 1) * ROWS, :] = own_ref[s, ROWS : 2 * ROWS, :]

    for s in range(BLOCKS):
        block = v_ref[s * ROWS : (s + 1) * ROWS, :].astype(F32).T.astype(BF16)
        turned[:, PAD + s * ROWS : PAD + (s + 1) * ROWS] = block
        vt_ref[:, s * ROWS : (s + 1) * ROWS] = block

    scale = DIM ** (-0.5) * math.log2(math.e)

    def rows(i, carry):
        q0 = i * SPAN
        query = jnp.concatenate([own_ref[2 * i, 0:ROWS, :], own_ref[2 * i + 1, 0:ROWS, :]], 0)
        first = scalar_start(q0, n_ref)
        last = scalar_start(q0 + SPAN - 1, n_ref)
        count = (q0 + SPAN - first + KEYS - 1) // KEYS
        q_at = q0 + lax.broadcasted_iota(jnp.int32, (1, SPAN), 1)
        start = doc_start(q_at, n_ref)

        def score(j, top):
            low = q0 + SPAN - (j + 1) * KEYS
            at = pl.multiple_of(low + PAD, SPAN)
            s = mm_nt(keys[pl.ds(at, KEYS), :], query)
            k_at = low + lax.broadcasted_iota(jnp.int32, (KEYS, SPAN), 0)
            s = jnp.where((k_at <= q_at) & (k_at >= start), s, NEG)
            scores[pl.ds(pl.multiple_of(j * KEYS, KEYS), KEYS), :] = s
            return jnp.maximum(top, jnp.max(s.reshape(KEYS // 8, 8, SPAN), axis=0))

        def score_plain(j, top):
            low = q0 + SPAN - (j + 1) * KEYS
            at = pl.multiple_of(low + PAD, SPAN)
            s = mm_nt(keys[pl.ds(at, KEYS), :], query)
            scores[pl.ds(pl.multiple_of(j * KEYS, KEYS), KEYS), :] = s
            return jnp.maximum(top, jnp.max(s.reshape(KEYS // 8, 8, SPAN), axis=0))

        top = score(0, jnp.full((8, SPAN), NEG, F32))
        inner = jnp.clip((q0 + SPAN - last) // KEYS, 1, count)
        top = lax.fori_loop(1, inner, score_plain, top)
        top = lax.fori_loop(inner, count, score, top)
        top = jnp.max(top, axis=0, keepdims=True)

        def mix(j, state):
            total, out = state
            low = q0 + SPAN - (j + 1) * KEYS
            at = pl.multiple_of(low + PAD, SPAN)
            s = scores[pl.ds(pl.multiple_of(j * KEYS, KEYS), KEYS), :]
            p = jnp.exp2((s - top) * scale)
            total = total + jnp.sum(p.reshape(KEYS // 8, 8, SPAN), axis=0)
            out = out + mm(turned[:, pl.ds(at, KEYS)], p.astype(BF16))
            return total, out

        total, out = lax.fori_loop(
            0, count, mix, (jnp.zeros((8, SPAN), F32), jnp.zeros((DIM, SPAN), F32))
        )
        total = jnp.sum(total, axis=0, keepdims=True)
        teach_ref[:, pl.ds(pl.multiple_of(q0, SPAN), SPAN)] = (out / total).astype(BF16)
        return carry

    lax.fori_loop(0, CHUNKS, rows, 0)


def attend(core, own, other):
    return pl.pallas_call(
        attend_kernel,
        out_shape=(
            jax.ShapeDtypeStruct((DIM, SEQ), BF16),
            jax.ShapeDtypeStruct((SEQ, DIM), BF16),
            jax.ShapeDtypeStruct((DIM, SEQ), BF16),
            jax.ShapeDtypeStruct((4,), jnp.int32),
        ),
        in_specs=[SMEM, VMEM, VMEM],
        out_specs=(VMEM, VMEM, VMEM, SMEM),
        scratch_shapes=[
            pltpu.VMEM((PAD + SEQ, DIM), BF16),
            pltpu.VMEM((DIM, PAD + SEQ), BF16),
            pltpu.VMEM((SEQ + KEYS, SPAN), F32),
        ],
        compiler_params=params(),
        cost_estimate=pl.CostEstimate(
            flops=8 << 30, bytes_accessed=8 << 20, transcendentals=8 << 20
        ),
    )(core, own, other)


def scan_lanes(x, reverse):
    width = x.shape[1]
    lane = lax.broadcasted_iota(jnp.int32, x.shape, 1)
    step = 1
    while step < width:
        if reverse:
            moved = pltpu.roll(x, width - step, 1)
            x = x + jnp.where(lane < width - step, moved, 0.0)
        else:
            moved = pltpu.roll(x, step, 1)
            x = x + jnp.where(lane >= step, moved, 0.0)
        step *= 2
    return x


def student_kernel(
    head_ref,
    n_ref,
    bias_ref,
    rate_ref,
    taps_ref,
    proj_ref,
    teach_ref,
    v_ref,
    vt_ref,
    out_ref,
    source,
    steps,
    cums,
    columns,
    pre_s,
    sig_s,
    z_s,
    dc_s,
    q_s,
    x_s,
    direct_s,
    state_s,
    dstate_s,
    *,
    weight,
):
    head = head_ref[0]
    group = head // SHARE
    bias = bias_ref[head]
    rate = rate_ref[head]
    lane = lax.broadcasted_iota(jnp.int32, (1, SPAN), 1)
    deep = lax.broadcasted_iota(jnp.int32, (SPAN, SPAN), 0)
    taps_b = taps_ref[pl.ds(pl.multiple_of(group * STATE, STATE), STATE), :]
    taps_c = taps_ref[pl.ds(pl.multiple_of(128 + group * STATE, STATE), STATE), :]
    taps = jnp.concatenate([taps_b, taps_c], 0)

    source[:, 0:128] = jnp.zeros((2 * STATE, 128), F32)
    for s in range(BLOCKS):
        source[:, 128 + s * ROWS : 128 + (s + 1) * ROWS] = proj_ref[s, 0 : 2 * STATE, :]
        steps[s // 2 : s // 2 + 1, (s % 2) * ROWS : (s % 2 + 1) * ROWS] = proj_ref[
            s, 2 * STATE : 2 * STATE + 1, :
        ]
    raw = steps[...] + bias
    step_all = jnp.maximum(raw, 0.0) + jnp.log1p(jnp.exp(-jnp.abs(raw)))
    slope_all = 1.0 / (1.0 + jnp.exp(-raw))
    steps[...] = step_all
    cum_all = scan_lanes(-step_all * rate, False)
    cums[...] = cum_all
    cum_turned = cum_all.T
    for c in range(CHUNKS):
        columns[c] = cum_turned[:, c : c + 1]

    def marks(c):
        base = c * SPAN
        at = base + lane
        start = doc_start(at, n_ref)
        last = scalar_start(base + SPAN - 1, n_ref)
        return base, at, start, last

    def forward(c, state):
        base, at, start, last = marks(c)
        wide = pl.multiple_of(base, SPAN)
        rows = source[:, pl.ds(wide, SPAN + 128)]
        pre = taps[:, 0:1] * rows[:, 128:]
        for j in range(1, TAPS):
            lagged = jnp.where(at - j >= start, pltpu.roll(rows, j, 1)[:, 128:], 0.0)
            pre = pre + taps[:, j : j + 1] * lagged
        sig = 1.0 / (1.0 + jnp.exp(-pre))
        gates = pre * sig
        pre_s[:, pl.ds(wide, SPAN)] = pre
        sig_s[:, pl.ds(wide, SPAN)] = sig
        gate_c = gates[STATE:]
        step = steps[pl.ds(c, 1), :]
        cum = cums[pl.ds(c, 1), :]
        ended = cum[:, SPAN - 1 :]
        fed = gates[:STATE] * step
        fed_high, fed_low = split(fed)
        c_high, c_low = split(gate_c)
        fed_stack = jnp.concatenate([fed, fed_low.astype(F32), fed], 0)
        left = fed_stack.T.astype(BF16)
        inner = mm(left, jnp.concatenate([c_high, c_high, c_low], 0))
        allowed = (deep <= lane) & (deep >= start - base)
        fade = jnp.exp(jnp.where(allowed, cum - columns[c], NEG))
        mixing = fade * inner
        mix_high, mix_low = split(mixing)
        values = v_ref[pl.ds(wide, SPAN), :]
        turned = vt_ref[:, pl.ds(wide, SPAN)]
        enter = jnp.where(start < base, jnp.exp(cum), 0.0)
        entered = gate_c * enter
        in_high, in_low = split(entered)
        s_high, s_low = split(state)
        state_left = jnp.concatenate([state, s_low.astype(F32), state], 0).T.astype(BF16)
        out = mm(turned, mix_high) + mm(turned, mix_low)
        out = out + mm(state_left, jnp.concatenate([in_high, in_high, in_low], 0))
        wanted = teach_ref[:, pl.ds(wide, SPAN)].astype(F32)
        error = (out - wanted) * weight
        q_s[pl.ds(c, 1), :] = jnp.sum(out * error, axis=0, keepdims=True)
        e_high, e_low = split(error)
        e_stack = jnp.concatenate([e_high, e_low], 0)
        pulled = fade * mm(jnp.concatenate([values, values], 1), e_stack)
        h_high, h_low = split(pulled)
        c_stack = jnp.concatenate([c_high, c_low], 0)
        z = mm_nt(c_stack, h_high) + mm_nt(c_stack, h_low)
        z_s[:, pl.ds(wide, SPAN)] = z[:STATE] + z[STATE:]
        fed_pair = jnp.concatenate([fed_high, fed_low], 0)
        dc = mm(fed_pair, h_high) + mm(fed_pair, h_low)
        s_pair = jnp.concatenate([s_high, s_low], 0)
        dc_in = mm(s_pair, e_high) + mm(s_pair, e_low)
        dc_s[:, pl.ds(wide, SPAN)] = dc[:STATE] + dc[STATE:] + enter * (dc_in[:STATE] + dc_in[STATE:])
        in_pair = jnp.concatenate([in_high, in_low], 0)
        ds = mm_nt(in_pair, e_high) + mm_nt(in_pair, e_low)
        dstate_s[c] = ds[:STATE] + ds[STATE:]
        state_s[c] = state
        tail = jnp.where(at >= last, jnp.exp(ended - cum), 0.0)
        t_high, t_low = split(fed * tail)
        new = mm(jnp.concatenate([t_high, t_low], 0), values)
        keep = jnp.where(last < base, 1.0, 0.0) * jnp.exp(ended)
        return keep * state + new[:STATE] + new[STATE:]

    final = lax.fori_loop(0, CHUNKS, forward, jnp.zeros((STATE, DIM), F32))
    state_s[CHUNKS] = final

    def backward(k, carried):
        dstate, later = carried
        c = CHUNKS - 1 - k
        base, at, start, last = marks(c)
        wide = pl.multiple_of(base, SPAN)
        step = steps[pl.ds(c, 1), :]
        cum = cums[pl.ds(c, 1), :]
        ended = cum[:, SPAN - 1 :]
        tail = jnp.where(at >= last, jnp.exp(ended - cum), 0.0)
        d_high, d_low = split(dstate)
        turned = vt_ref[:, pl.ds(wide, SPAN)]
        through = mm(jnp.concatenate([d_high, d_low], 0), turned)
        z = z_s[:, pl.ds(wide, SPAN)] + tail * (through[:STATE] + through[STATE:])
        pre = pre_s[:, pl.ds(wide, SPAN)]
        sig = sig_s[:, pl.ds(wide, SPAN)]
        gates = pre * sig
        direct = jnp.sum(gates[:STATE] * z, axis=0, keepdims=True)
        direct_s[pl.ds(c, 1), :] = direct
        crossing = jnp.sum(jnp.sum(dstate * state_s[c + 1], axis=0, keepdims=True), axis=1, keepdims=True)
        x_s[pl.ds(c, 1), :] = jnp.broadcast_to(crossing, (1, SPAN))
        dgates = jnp.concatenate([step * z, dc_s[:, pl.ds(wide, SPAN)]], 0)
        dpre = dgates * (sig + gates * (1.0 - sig))
        rows = jnp.concatenate([dpre, later], 1)
        back = taps[:, 0:1] * rows[:, :SPAN]
        for j in range(1, TAPS):
            reach = jnp.where(at >= doc_start(at + j, n_ref), pltpu.roll(rows, SPAN + 128 - j, 1)[:, :SPAN], 0.0)
            back = back + taps[:, j : j + 1] * reach
        column = pl.multiple_of((c // 2) * ROWS, ROWS)
        out_ref[2 * (c % 2), 0 : 2 * STATE, pl.ds(column, ROWS)] = back[:, :ROWS]
        out_ref[2 * (c % 2) + 1, 0 : 2 * STATE, pl.ds(column, ROWS)] = back[:, ROWS:]
        keep = jnp.where(last < base, 1.0, 0.0) * jnp.exp(ended)
        return keep * dstate + dstate_s[c], dpre[:, :128]

    nothing = (jnp.zeros((STATE, DIM), F32), jnp.zeros((2 * STATE, 128), F32))
    lax.fori_loop(0, CHUNKS, backward, nothing)

    at_all = lax.broadcasted_iota(jnp.int32, (CHUNKS, SPAN), 0) * SPAN
    at_all = at_all + lax.broadcasted_iota(jnp.int32, (CHUNKS, SPAN), 1)
    direct = direct_s[...]
    dlog = scan_lanes(q_s[...] - step_all * direct, True) + x_s[...]
    dlog = jnp.where(at_all > doc_start(at_all, n_ref), dlog, 0.0)
    dstep = (direct - rate * dlog) * slope_all
    for s in range(BLOCKS):
        piece = dstep[s // 2 : s // 2 + 1, (s % 2) * ROWS : (s % 2 + 1) * ROWS]
        out_ref[s % SHARE, 2 * STATE :, (s // SHARE) * ROWS : (s // SHARE + 1) * ROWS] = (
            jnp.broadcast_to(piece, (COLS - 2 * STATE, ROWS))
        )


def student(head, counts, bias, rate, taps, proj, teach, v, vt, weight):
    return pl.pallas_call(
        lambda *refs: student_kernel(*refs, weight=weight),
        out_shape=jax.ShapeDtypeStruct((SHARE, COLS, QUARTER), F32),
        in_specs=[SMEM, SMEM, SMEM, SMEM, VMEM, VMEM, VMEM, VMEM, VMEM],
        out_specs=VMEM,
        scratch_shapes=[
            pltpu.VMEM((2 * STATE, 128 + SEQ), F32),
            pltpu.VMEM((CHUNKS, SPAN), F32),
            pltpu.VMEM((CHUNKS, SPAN), F32),
            pltpu.VMEM((CHUNKS, SPAN, 1), F32),
            pltpu.VMEM((2 * STATE, SEQ), F32),
            pltpu.VMEM((2 * STATE, SEQ), F32),
            pltpu.VMEM((STATE, SEQ), F32),
            pltpu.VMEM((STATE, SEQ), F32),
            pltpu.VMEM((CHUNKS, SPAN), F32),
            pltpu.VMEM((CHUNKS, SPAN), F32),
            pltpu.VMEM((CHUNKS, SPAN), F32),
            pltpu.VMEM((CHUNKS + 1, STATE, DIM), F32),
            pltpu.VMEM((CHUNKS, STATE, DIM), F32),
        ],
        compiler_params=params(),
        cost_estimate=pl.CostEstimate(
            flops=8 << 30, bytes_accessed=8 << 20, transcendentals=4 << 20
        ),
    )(head, counts, bias, rate, taps, proj, teach, v, vt)


def combine_kernel(in_ref, out_ref):
    gates = in_ref[0, : 2 * STATE] + in_ref[1, : 2 * STATE]
    gates = gates + in_ref[2, : 2 * STATE]
    gates = gates + in_ref[3, : 2 * STATE]
    steps = [in_ref[k, 2 * STATE : 2 * STATE + 1] for k in range(SHARE)]
    rest = jnp.zeros((COLS - 2 * STATE - SHARE, QUARTER), F32)
    rounded = jnp.concatenate([gates] + steps + [rest], 0).astype(BF16)
    for g in range(GROUPS):
        out_ref[g] = rounded


def combine(parts):
    return pl.pallas_call(
        combine_kernel,
        out_shape=jax.ShapeDtypeStruct((GROUPS, COLS, QUARTER), BF16),
        in_specs=[VMEM],
        out_specs=VMEM,
        compiler_params=params(32),
    )(parts)


def product_kernel(place_ref, own_ref, other_ref, hid_ref, keep_ref, send_ref, left):
    core = place_ref[0]
    pair = place_ref[1]
    for k, ref in enumerate((own_ref, other_ref)):
        for half in range(2):
            rows = [ref[4 * half + i].astype(F32) for i in range(4)]
            left[k, half] = jnp.concatenate(rows, 0).astype(BF16)
    own_hid = hid_ref[:, core].reshape(QUARTER, 512)
    other_hid = hid_ref[:, 1 - core].reshape(QUARTER, 512)
    for ref, half in ((send_ref, 1 - pair), (keep_ref, pair)):
        part = mm(left[0, half], own_hid) + mm(left[1, half], other_hid)
        for i in range(4):
            for r in range(2):
                ref[r, i] = part[r * 80 : (r + 1) * 80, i * 128 : (i + 1) * 128]


def product(place, own, other, hidden):
    shape = jax.ShapeDtypeStruct((2, PARTS // 2, 2 * COLS, 128), F32)
    return pl.pallas_call(
        product_kernel,
        out_shape=(shape, shape),
        in_specs=[SMEM, VMEM, VMEM, VMEM],
        out_specs=(VMEM, VMEM),
        scratch_shapes=[pltpu.VMEM((2, 2, 4 * COLS, QUARTER), BF16)],
        compiler_params=params(32),
        cost_estimate=pl.CostEstimate(
            flops=2 * 320 * 1024 * 1024, bytes_accessed=4 << 20, transcendentals=0
        ),
    )(place, own, other, hidden.reshape(GROUPS, 2, ROWS, 512))


def arrange_kernel(core_ref, own_ref, other_ref, out_ref):
    first = core_ref[0] == 0
    for g in range(GROUPS):
        lanes = slice(g * 128, (g + 1) * 128)
        for k in range(GROUPS):
            at = 2 * g + k // 4
            mine, theirs = own_ref[at], other_ref[at]
            rows = slice((k % 2) * COLS, (k % 2 + 1) * COLS)
            if (k // 2) % 2 == 0:
                block = jnp.where(first, mine[rows], theirs[rows])
            else:
                block = jnp.where(first, theirs[rows], mine[rows])
            out_ref[k * STATE : (k + 1) * STATE, lanes] = block[:STATE]
            out_ref[128 + k * STATE : 128 + (k + 1) * STATE, lanes] = block[STATE : 2 * STATE]
            steps = block[2 * STATE : 2 * STATE + SHARE]
            out_ref[256 + k * SHARE : 256 + (k + 1) * SHARE, lanes] = steps


def arrange(core, own, other):
    return pl.pallas_call(
        arrange_kernel,
        out_shape=jax.ShapeDtypeStruct((288, 1024), F32),
        in_specs=[SMEM, VMEM, VMEM],
        out_specs=VMEM,
        compiler_params=params(32),
    )(core, own, other)


def swap_all(x, axis, groups=None):
    return lax.all_to_all(x, axis, 0, 0, tiled=True, axis_index_groups=groups)


def local(hidden, queries, keys, values, docs, w_proj, conv_weight, dt_bias, decay_rate):
    seq_devices = lax.axis_size("seq")
    data_devices = lax.axis_size("dp")
    seq_len = hidden.shape[1] * seq_devices
    weight = 1.0 / math.sqrt(HEADS * DIM * data_devices * seq_len)
    head = lax.axis_index("seq").astype(jnp.int32)
    core = lax.rem(head, 2)
    pair = lax.rem(lax.div(head, 2), 2)
    twos = [[2 * i, 2 * i + 1] for i in range(seq_devices // 2)]
    fours = [[SHARE * g + j for j in range(SHARE)] for g in range(GROUPS)]
    eights = [[SHARE * g + j for g in range(GROUPS)] for j in range(SHARE)]
    halves = [[SHARE * g + 2 * y + c for g in range(GROUPS) for c in range(2)] for y in range(2)]
    same_core = [[SHARE * g + 2 * y + c for g in range(GROUPS) for y in range(2)] for c in range(2)]
    partner = [(i, i ^ 1) for i in range(seq_devices)]
    across = [(i, i ^ 2) for i in range(seq_devices)]

    turned_w = w_proj.T
    half = turned_w.shape[1] // 2
    own_w = lax.dynamic_slice_in_dim(turned_w, core * half, half, 1)
    own_w = lax.all_gather(own_w, "dp", axis=0)
    other_w = lax.ppermute(own_w, "seq", partner)

    own = swap_all(pack_teacher(queries, keys, values, docs), "seq")
    other = lax.ppermute(own[:, ROWS : 2 * ROWS, :], "seq", partner)
    proj = swap_all(project(core[None], hidden, own_w, other_w), "seq")
    teach, v, vt, counts = attend(core[None], own, other)
    hidden_packed = pack_hidden(hidden)
    hidden_packed, proj = lax.optimization_barrier((hidden_packed, proj))
    hidden_part = swap_all(hidden_packed, "seq", halves)
    grads = student(
        head[None], counts, dt_bias, decay_rate, conv_weight.T, proj, teach, v, vt, weight
    )
    grads, hidden_part = lax.optimization_barrier((grads, hidden_part))
    own_grads = swap_all(combine(swap_all(grads, "seq", fours)), "seq", eights)
    other_grads = lax.ppermute(own_grads, "seq", partner)
    keep, send = product(jnp.stack([core, pair]), own_grads, other_grads, hidden_part)
    summed = keep + lax.ppermute(send, "seq", across)
    rows = swap_all(summed, "seq", twos).reshape(PARTS, 2 * COLS, 128)
    total = jnp.sum(swap_all(rows, "dp"), axis=0)
    spread = jnp.broadcast_to(total[None], (seq_devices // 2, 2 * COLS, 128))
    own_blocks = swap_all(spread, "seq", same_core)
    other_blocks = lax.ppermute(own_blocks, "seq", partner)
    return arrange(core[None], own_blocks, other_blocks).T


def solution(mesh):
    placed = (
        P("dp", "seq", None),
        P("dp", "seq", None),
        P("dp", "seq", None),
        P("dp", "seq", None),
        P("dp", "seq"),
        P("dp", None),
        P(),
        P(),
        P(),
    )
    return jax.shard_map(
        local, mesh=mesh, in_specs=placed, out_specs=P("dp", None), check_vma=False
    )
```

```python
import math

import jax
import jax.numpy as jnp
from jax import lax
from jax.experimental import pallas as pl
from jax.experimental.pallas import tpu as pltpu
from jax.sharding import PartitionSpec as P

D = 8192
HEADS = 32
GROUPS = 8
SHARE = 4
DIM = 128
STATE = 16
TAPS = 4
SEQ = 4096
ROWS = 128
BLOCKS = SEQ // ROWS
PARTS = 8
WIDTH = 288
DOC_ROWS = 16
TEACH_ROWS = 2 * ROWS + DOC_ROWS
COLS = 40
SPAN = 256
CHUNKS = SEQ // SPAN
KEYS = 1024
HALF = KEYS // 2
QUERIES = 512
PAD = max(0, KEYS - QUERIES)
UNROLL = 16
PACK_STEPS = 2
PROJECT_STEPS = 2

F32 = jnp.float32
BF16 = jnp.bfloat16
NEG = -1e30
VMEM = pl.BlockSpec(memory_space=pltpu.VMEM)
SMEM = pl.BlockSpec(memory_space=pltpu.SMEM)

NT = (((1,), (1,)), ((), ()))


def params(mib=56):
    return pltpu.CompilerParams(vmem_limit_bytes=mib << 20)


def mm(a, b):
    return jnp.dot(a, b, preferred_element_type=F32)


def mm_nt(a, b):
    return lax.dot_general(a, b, NT, preferred_element_type=F32)


def split(x):
    high = x.astype(BF16)
    return high, (x - high.astype(F32)).astype(BF16)


def doc_start(position, n_ref):
    start = jnp.where(position >= n_ref[0], n_ref[0], 0)
    start = jnp.where(position >= n_ref[1], n_ref[1], start)
    return jnp.where(position >= n_ref[2], n_ref[2], start)


def scalar_start(position, n_ref):
    return doc_start(position, n_ref)


def pack_teacher_kernel(q_ref, k_ref, v_ref, doc_ref, out_ref):
    docs = jnp.broadcast_to(doc_ref[...].astype(F32), (DOC_ROWS, ROWS)).astype(BF16)
    for k in range(q_ref.shape[2] // DIM):
        g = k // SHARE
        out_ref[k, 0:ROWS, :] = q_ref[0, :, k * DIM : (k + 1) * DIM]
        source = k_ref if k % 2 == 0 else v_ref
        out_ref[k, ROWS : 2 * ROWS, :] = source[0, :, g * DIM : (g + 1) * DIM]
        out_ref[k, 2 * ROWS :, :] = docs


def pack_teacher(q, k, v, docs):
    many = GROUPS // PACK_STEPS
    return pl.pallas_call(
        pack_teacher_kernel,
        out_shape=jax.ShapeDtypeStruct((HEADS, TEACH_ROWS, DIM), BF16),
        grid=(PACK_STEPS,),
        in_specs=[
            pl.BlockSpec((1, ROWS, many * SHARE * DIM), lambda g: (0, 0, g)),
            pl.BlockSpec((1, ROWS, many * DIM), lambda g: (0, 0, g)),
            pl.BlockSpec((1, ROWS, many * DIM), lambda g: (0, 0, g)),
            pl.BlockSpec((1, ROWS), lambda g: (0, 0)),
        ],
        out_specs=pl.BlockSpec((many * SHARE, TEACH_ROWS, DIM), lambda g: (g, 0, 0)),
        compiler_params=params(60),
        cost_estimate=pl.CostEstimate(flops=0, bytes_accessed=4 << 20, transcendentals=0),
    )(q, k, v, docs)


def pack_hidden_kernel(part_ref, hid_ref, *out_refs):
    width = out_refs[0].shape[1]
    for k, ref in enumerate(out_refs):
        block = lax.rem(part_ref[0] + k, PARTS)
        ref[...] = hid_ref[0, :, pl.ds(pl.multiple_of(block * width, width), width)]


def pack_hidden(part, hidden):
    block = jax.ShapeDtypeStruct((ROWS, D // PARTS), BF16)
    return pl.pallas_call(
        pack_hidden_kernel,
        out_shape=(block,) * PARTS,
        in_specs=[SMEM, VMEM],
        out_specs=(VMEM,) * PARTS,
        compiler_params=params(60),
        cost_estimate=pl.CostEstimate(flops=0, bytes_accessed=4 << 20, transcendentals=0),
    )(part, hidden)


def project_kernel(core_ref, hid_ref, own_ref, other_ref, out_ref, acc_ref):
    step = pl.program_id(0)
    many, _, half = own_ref.shape
    part = 0.0
    for i in range(many):
        mine = pl.multiple_of((2 * i + core_ref[0]) * half, half)
        theirs = pl.multiple_of((2 * i + 1 - core_ref[0]) * half, half)
        part = part + mm_nt(own_ref[i], hid_ref[0, :, pl.ds(mine, half)])
        part = part + mm_nt(other_ref[i], hid_ref[0, :, pl.ds(theirs, half)])

    @pl.when(step == 0)
    def _():
        acc_ref[...] = part

    @pl.when(step > 0)
    def _():
        acc_ref[...] += part

    @pl.when(step == PROJECT_STEPS - 1)
    def _():
        for h in range(HEADS):
            g = h // SHARE
            out_ref[h, 0:STATE, :] = acc_ref[g * STATE : (g + 1) * STATE]
            out_ref[h, STATE : 2 * STATE, :] = acc_ref[128 + g * STATE : 128 + (g + 1) * STATE]
            out_ref[h, 2 * STATE :, :] = jnp.broadcast_to(
                acc_ref[256 + h : 257 + h], (COLS - 2 * STATE, ROWS)
            )


def project(core, hidden, own, other):
    _, width, half = own.shape
    many = PARTS // PROJECT_STEPS
    return pl.pallas_call(
        project_kernel,
        out_shape=jax.ShapeDtypeStruct((HEADS, COLS, ROWS), F32),
        grid_spec=pltpu.PrefetchScalarGridSpec(
            num_scalar_prefetch=1,
            grid=(PROJECT_STEPS,),
            in_specs=[
                pl.BlockSpec((1, ROWS, many * 2 * half), lambda i, c: (0, 0, i)),
                pl.BlockSpec((many, width, half), lambda i, c: (i, 0, 0)),
                pl.BlockSpec((many, width, half), lambda i, c: (i, 0, 0)),
            ],
            out_specs=pl.BlockSpec((HEADS, COLS, ROWS), lambda i, c: (0, 0, 0)),
            scratch_shapes=[pltpu.VMEM((width, ROWS), F32)],
        ),
        compiler_params=params(60),
        cost_estimate=pl.CostEstimate(
            flops=2 * ROWS * D * 288, bytes_accessed=8 << 20, transcendentals=0
        ),
    )(core, hidden, own, other)


def attend_kernel(
    core_ref, own_ref, other_ref, teach_ref, v_ref, vt_ref, n_ref, keys, turned, scores
):
    docs = jnp.max(own_ref[:, 2 * ROWS :, :].astype(F32), axis=1)
    for d in range(3):
        n_ref[d] = jnp.sum((docs < d + 0.5).astype(F32)).astype(jnp.int32)
    n_ref[3] = 0
    if PAD:
        keys[0:PAD, :] = jnp.zeros((PAD, DIM), BF16)
        turned[:, 0:PAD] = jnp.zeros((DIM, PAD), BF16)

    @pl.when(core_ref[0] == 0)
    def _():
        for s in range(BLOCKS):
            keys[PAD + s * ROWS : PAD + (s + 1) * ROWS, :] = own_ref[s, ROWS : 2 * ROWS, :]
            v_ref[s * ROWS : (s + 1) * ROWS, :] = other_ref[s]

    @pl.when(core_ref[0] != 0)
    def _():
        for s in range(BLOCKS):
            keys[PAD + s * ROWS : PAD + (s + 1) * ROWS, :] = other_ref[s]
            v_ref[s * ROWS : (s + 1) * ROWS, :] = own_ref[s, ROWS : 2 * ROWS, :]

    for s in range(BLOCKS):
        block = v_ref[s * ROWS : (s + 1) * ROWS, :].T
        turned[:, PAD + s * ROWS : PAD + (s + 1) * ROWS] = block
        vt_ref[:, s * ROWS : (s + 1) * ROWS] = block

    scale = DIM ** (-0.5) * math.log2(math.e)

    def rows(i, carry):
        q0 = i * QUERIES
        many = QUERIES // ROWS
        query = jnp.concatenate([own_ref[many * i + k, 0:ROWS, :] for k in range(many)], 0)
        first = scalar_start(q0, n_ref)
        last = scalar_start(q0 + QUERIES - 1, n_ref)
        need = q0 + QUERIES - first
        rest = lax.rem(need, KEYS)
        count = need // KEYS + (rest > HALF).astype(jnp.int32)
        ends = ((rest > 0) & (rest <= HALF)).astype(jnp.int32)
        q_at = q0 + lax.broadcasted_iota(jnp.int32, (1, QUERIES), 1)
        start = doc_start(q_at, n_ref)

        def tile(at, size):
            low = q0 + QUERIES - at - size
            return low, pl.multiple_of(low + PAD, HALF), pl.ds(pl.multiple_of(at, HALF), size)

        def score(at, size, masked, top):
            low, key_at, rows_at = tile(at, size)
            s = mm_nt(keys[pl.ds(key_at, size), :], query)
            if masked:
                k_at = low + lax.broadcasted_iota(jnp.int32, (size, QUERIES), 0)
                s = jnp.where((k_at <= q_at) & (k_at >= start), s, NEG)
            scores[rows_at, :] = s
            return jnp.maximum(top, jnp.max(s.reshape(size // 8, 8, QUERIES), axis=0))

        def masked(j, top):
            return score(j * KEYS, KEYS, True, top)

        def plain(j, top):
            return score(j * KEYS, KEYS, False, top)

        def masked_half(j, top):
            return score(count * KEYS, HALF, True, top)

        one = jnp.minimum(count, 1)
        inner = jnp.clip((q0 + QUERIES - last) // KEYS, one, count)
        top = jnp.full((8, QUERIES), NEG, F32)
        top = lax.fori_loop(0, one, masked, top)
        top = lax.fori_loop(one, inner, plain, top)
        top = lax.fori_loop(inner, count, masked, top)
        top = lax.fori_loop(0, ends, masked_half, top)
        top = jnp.max(top, axis=0, keepdims=True)

        def mix(at, size, state):
            total, out = state
            _, key_at, rows_at = tile(at, size)
            p = jnp.exp2((scores[rows_at, :] - top) * scale)
            total = total + jnp.sum(p.reshape(size // 8, 8, QUERIES), axis=0)
            return total, out + mm(turned[:, pl.ds(key_at, size)], p.astype(BF16))

        state = (jnp.zeros((8, QUERIES), F32), jnp.zeros((DIM, QUERIES), F32))
        state = lax.fori_loop(0, count, lambda j, t: mix(j * KEYS, KEYS, t), state)
        total, out = lax.fori_loop(0, ends, lambda j, t: mix(count * KEYS, HALF, t), state)
        total = jnp.sum(total, axis=0, keepdims=True)
        teach_ref[:, pl.ds(pl.multiple_of(q0, QUERIES), QUERIES)] = (out / total).astype(BF16)
        return carry

    lax.fori_loop(0, SEQ // QUERIES, rows, 0)


def attend(core, own, other):
    return pl.pallas_call(
        attend_kernel,
        out_shape=(
            jax.ShapeDtypeStruct((DIM, SEQ), BF16),
            jax.ShapeDtypeStruct((SEQ, DIM), BF16),
            jax.ShapeDtypeStruct((DIM, SEQ), BF16),
            jax.ShapeDtypeStruct((4,), jnp.int32),
        ),
        in_specs=[SMEM, VMEM, VMEM],
        out_specs=(VMEM, VMEM, VMEM, SMEM),
        scratch_shapes=[
            pltpu.VMEM((PAD + SEQ, DIM), BF16),
            pltpu.VMEM((DIM, PAD + SEQ), BF16),
            pltpu.VMEM((SEQ + KEYS, QUERIES), F32),
        ],
        compiler_params=params(56),
        cost_estimate=pl.CostEstimate(
            flops=8 << 30, bytes_accessed=8 << 20, transcendentals=8 << 20
        ),
    )(core, own, other)


def scan_lanes(x, reverse):
    width = x.shape[1]
    lane = lax.broadcasted_iota(jnp.int32, x.shape, 1)
    step = 1
    while step < width:
        if reverse:
            moved = pltpu.roll(x, width - step, 1)
            x = x + jnp.where(lane < width - step, moved, 0.0)
        else:
            moved = pltpu.roll(x, step, 1)
            x = x + jnp.where(lane >= step, moved, 0.0)
        step *= 2
    return x


def student_kernel(
    head_ref,
    n_ref,
    bias_ref,
    rate_ref,
    taps_ref,
    proj_ref,
    teach_ref,
    v_ref,
    vt_ref,
    out_ref,
    source,
    steps,
    cums,
    columns,
    pre_s,
    sig_s,
    z_s,
    dc_s,
    q_s,
    x_s,
    direct_s,
    state_s,
    dstate_s,
    *,
    weight,
):
    head = head_ref[0]
    group = head // SHARE
    bias = bias_ref[head]
    rate = rate_ref[head]
    lane = lax.broadcasted_iota(jnp.int32, (1, SPAN), 1)
    deep = lax.broadcasted_iota(jnp.int32, (SPAN, SPAN), 0)
    taps_b = taps_ref[pl.ds(pl.multiple_of(group * STATE, STATE), STATE), :]
    taps_c = taps_ref[pl.ds(pl.multiple_of(128 + group * STATE, STATE), STATE), :]
    taps = jnp.concatenate([taps_b, taps_c], 0)

    source[:, 0:128] = jnp.zeros((2 * STATE, 128), F32)
    for s in range(BLOCKS):
        source[:, 128 + s * ROWS : 128 + (s + 1) * ROWS] = proj_ref[s, 0 : 2 * STATE, :]
        steps[s // 2 : s // 2 + 1, (s % 2) * ROWS : (s % 2 + 1) * ROWS] = proj_ref[
            s, 2 * STATE : 2 * STATE + 1, :
        ]
    raw = steps[...] + bias
    step_all = jnp.maximum(raw, 0.0) + jnp.log1p(jnp.exp(-jnp.abs(raw)))
    slope_all = 1.0 / (1.0 + jnp.exp(-raw))
    steps[...] = step_all
    cum_all = scan_lanes(-step_all * rate, False)
    cums[...] = cum_all
    cum_turned = cum_all.T
    for c in range(CHUNKS):
        columns[c] = cum_turned[:, c : c + 1]

    def marks(c):
        base = c * SPAN
        at = base + lane
        start = doc_start(at, n_ref)
        last = scalar_start(base + SPAN - 1, n_ref)
        return base, at, start, last

    def forward(c, state):
        base, at, start, last = marks(c)
        wide = pl.multiple_of(base, SPAN)
        rows = source[:, pl.ds(wide, SPAN + 128)]
        pre = taps[:, 0:1] * rows[:, 128:]
        for j in range(1, TAPS):
            lagged = jnp.where(at - j >= start, pltpu.roll(rows, j, 1)[:, 128:], 0.0)
            pre = pre + taps[:, j : j + 1] * lagged
        sig = 1.0 / (1.0 + jnp.exp(-pre))
        gates = pre * sig
        pre_s[:, pl.ds(wide, SPAN)] = pre
        sig_s[:, pl.ds(wide, SPAN)] = sig
        gate_c = gates[STATE:]
        step = steps[pl.ds(c, 1), :]
        cum = cums[pl.ds(c, 1), :]
        ended = cum[:, SPAN - 1 :]
        fed = gates[:STATE] * step
        fed_high, fed_low = split(fed)
        c_high, c_low = split(gate_c)
        fed_stack = jnp.concatenate([fed, fed_low.astype(F32), fed], 0)
        left = fed_stack.T.astype(BF16)
        inner = mm(left, jnp.concatenate([c_high, c_high, c_low], 0))
        allowed = (deep <= lane) & (deep >= start - base)
        fade = jnp.exp(jnp.where(allowed, cum - columns[c], NEG))
        mixing = fade * inner
        mix_high, mix_low = split(mixing)
        values = v_ref[pl.ds(wide, SPAN), :]
        turned = vt_ref[:, pl.ds(wide, SPAN)]
        enter = jnp.where(start < base, jnp.exp(cum), 0.0)
        entered = gate_c * enter
        in_high, in_low = split(entered)
        s_high, s_low = split(state)
        state_left = jnp.concatenate([state, s_low.astype(F32), state], 0).T.astype(BF16)
        out = mm(turned, mix_high) + mm(turned, mix_low)
        out = out + mm(state_left, jnp.concatenate([in_high, in_high, in_low], 0))
        wanted = teach_ref[:, pl.ds(wide, SPAN)].astype(F32)
        error = (out - wanted) * weight
        q_s[pl.ds(c, 1), :] = jnp.sum(out * error, axis=0, keepdims=True)
        e_high, e_low = split(error)
        e_stack = jnp.concatenate([e_high, e_low], 0)
        pulled = fade * mm(jnp.concatenate([values, values], 1), e_stack)
        h_high, h_low = split(pulled)
        c_stack = jnp.concatenate([c_high, c_low], 0)
        z = mm_nt(c_stack, h_high) + mm_nt(c_stack, h_low)
        z_s[:, pl.ds(wide, SPAN)] = z[:STATE] + z[STATE:]
        fed_pair = jnp.concatenate([fed_high, fed_low], 0)
        dc = mm(fed_pair, h_high) + mm(fed_pair, h_low)
        s_pair = jnp.concatenate([s_high, s_low], 0)
        dc_in = mm(s_pair, e_high) + mm(s_pair, e_low)
        dc_s[:, pl.ds(wide, SPAN)] = dc[:STATE] + dc[STATE:] + enter * (dc_in[:STATE] + dc_in[STATE:])
        in_pair = jnp.concatenate([in_high, in_low], 0)
        ds = mm_nt(in_pair, e_high) + mm_nt(in_pair, e_low)
        dstate_s[c] = ds[:STATE] + ds[STATE:]
        state_s[c] = state
        tail = jnp.where(at >= last, jnp.exp(ended - cum), 0.0)
        t_high, t_low = split(fed * tail)
        new = mm(jnp.concatenate([t_high, t_low], 0), values)
        keep = jnp.where(last < base, 1.0, 0.0) * jnp.exp(ended)
        return keep * state + new[:STATE] + new[STATE:]

    final = lax.fori_loop(0, CHUNKS, forward, jnp.zeros((STATE, DIM), F32), unroll=UNROLL)
    state_s[CHUNKS] = final

    def backward(k, carried):
        dstate, later = carried
        c = CHUNKS - 1 - k
        base, at, start, last = marks(c)
        wide = pl.multiple_of(base, SPAN)
        step = steps[pl.ds(c, 1), :]
        cum = cums[pl.ds(c, 1), :]
        ended = cum[:, SPAN - 1 :]
        tail = jnp.where(at >= last, jnp.exp(ended - cum), 0.0)
        d_high, d_low = split(dstate)
        turned = vt_ref[:, pl.ds(wide, SPAN)]
        through = mm(jnp.concatenate([d_high, d_low], 0), turned)
        z = z_s[:, pl.ds(wide, SPAN)] + tail * (through[:STATE] + through[STATE:])
        pre = pre_s[:, pl.ds(wide, SPAN)]
        sig = sig_s[:, pl.ds(wide, SPAN)]
        gates = pre * sig
        direct = jnp.sum(gates[:STATE] * z, axis=0, keepdims=True)
        direct_s[pl.ds(c, 1), :] = direct
        crossing = jnp.sum(jnp.sum(dstate * state_s[c + 1], axis=0, keepdims=True), axis=1, keepdims=True)
        x_s[pl.ds(c, 1), :] = jnp.broadcast_to(crossing, (1, SPAN))
        dgates = jnp.concatenate([step * z, dc_s[:, pl.ds(wide, SPAN)]], 0)
        dpre = dgates * (sig + gates * (1.0 - sig))
        rows = jnp.concatenate([dpre, later], 1)
        back = taps[:, 0:1] * rows[:, :SPAN]
        for j in range(1, TAPS):
            reach = jnp.where(at >= doc_start(at + j, n_ref), pltpu.roll(rows, SPAN + 128 - j, 1)[:, :SPAN], 0.0)
            back = back + taps[:, j : j + 1] * reach
        out_ref[2 * c, 0 : 2 * STATE, :] = back[:, :ROWS]
        out_ref[2 * c + 1, 0 : 2 * STATE, :] = back[:, ROWS:]
        keep = jnp.where(last < base, 1.0, 0.0) * jnp.exp(ended)
        return keep * dstate + dstate_s[c], dpre[:, :128]

    nothing = (jnp.zeros((STATE, DIM), F32), jnp.zeros((2 * STATE, 128), F32))
    lax.fori_loop(0, CHUNKS, backward, nothing, unroll=UNROLL)

    at_all = lax.broadcasted_iota(jnp.int32, (CHUNKS, SPAN), 0) * SPAN
    at_all = at_all + lax.broadcasted_iota(jnp.int32, (CHUNKS, SPAN), 1)
    direct = direct_s[...]
    dlog = scan_lanes(q_s[...] - step_all * direct, True) + x_s[...]
    dlog = jnp.where(at_all > doc_start(at_all, n_ref), dlog, 0.0)
    dstep = (direct - rate * dlog) * slope_all
    for s in range(BLOCKS):
        piece = dstep[s // 2 : s // 2 + 1, (s % 2) * ROWS : (s % 2 + 1) * ROWS]
        out_ref[s, 2 * STATE :, :] = jnp.broadcast_to(piece, (COLS - 2 * STATE, ROWS))


def student(head, counts, bias, rate, taps, proj, teach, v, vt, weight):
    return pl.pallas_call(
        lambda *refs: student_kernel(*refs, weight=weight),
        out_shape=jax.ShapeDtypeStruct((BLOCKS, COLS, ROWS), F32),
        in_specs=[SMEM, SMEM, SMEM, SMEM, VMEM, VMEM, VMEM, VMEM, VMEM],
        out_specs=VMEM,
        scratch_shapes=[
            pltpu.VMEM((2 * STATE, 128 + SEQ), F32),
            pltpu.VMEM((CHUNKS, SPAN), F32),
            pltpu.VMEM((CHUNKS, SPAN), F32),
            pltpu.VMEM((CHUNKS, SPAN, 1), F32),
            pltpu.VMEM((2 * STATE, SEQ), F32),
            pltpu.VMEM((2 * STATE, SEQ), F32),
            pltpu.VMEM((STATE, SEQ), F32),
            pltpu.VMEM((STATE, SEQ), F32),
            pltpu.VMEM((CHUNKS, SPAN), F32),
            pltpu.VMEM((CHUNKS, SPAN), F32),
            pltpu.VMEM((CHUNKS, SPAN), F32),
            pltpu.VMEM((CHUNKS + 1, STATE, DIM), F32),
            pltpu.VMEM((CHUNKS, STATE, DIM), F32),
        ],
        compiler_params=params(56),
        cost_estimate=pl.CostEstimate(
            flops=8 << 30, bytes_accessed=8 << 20, transcendentals=4 << 20
        ),
    )(head, counts, bias, rate, taps, proj, teach, v, vt)


def combine_kernel(in_ref, out_ref, rows):
    for g in range(GROUPS):
        gates = in_ref[SHARE * g, : 2 * STATE]
        for k in range(1, SHARE):
            gates = gates + in_ref[SHARE * g + k, : 2 * STATE]
        rows[g * STATE : (g + 1) * STATE] = gates[:STATE]
        rows[128 + g * STATE : 128 + (g + 1) * STATE] = gates[STATE:]
    for h in range(HEADS):
        rows[256 + h : 257 + h] = in_ref[h, 2 * STATE : 2 * STATE + 1]
    rounded = rows[...].astype(BF16)
    for d in range(PARTS):
        out_ref[d] = rounded


def combine(parts):
    return pl.pallas_call(
        combine_kernel,
        out_shape=jax.ShapeDtypeStruct((PARTS, WIDTH, ROWS), BF16),
        in_specs=[VMEM],
        out_specs=VMEM,
        scratch_shapes=[pltpu.VMEM((WIDTH, ROWS), F32)],
        compiler_params=params(16),
    )(parts)


def product_kernel(core_ref, part_ref, grad_ref, *refs):
    blocks, (keep_ref, send_ref) = refs[:PARTS], refs[PARTS:]
    left = jnp.concatenate(
        [grad_ref[lax.rem(part_ref[0] + PARTS - k, PARTS)] for k in range(PARTS)], 1
    )
    half = blocks[0].shape[1] // 2
    for ref, core in ((send_ref, 1 - core_ref[0]), (keep_ref, core_ref[0])):
        lanes = pl.ds(pl.multiple_of(core * half, half), half)
        part = mm(left, jnp.concatenate([block[:, lanes] for block in blocks], 0))
        for r in range(4):
            for q in range(4):
                ref[4 * r + q] = part[r * 72 : (r + 1) * 72, q * 128 : (q + 1) * 128]


def product(core, part, grads, blocks):
    shape = jax.ShapeDtypeStruct((16, WIDTH // 4, 128), F32)
    return pl.pallas_call(
        product_kernel,
        out_shape=(shape, shape),
        in_specs=[SMEM, SMEM, VMEM] + [VMEM] * PARTS,
        out_specs=(VMEM, VMEM),
        compiler_params=params(24),
        cost_estimate=pl.CostEstimate(
            flops=2 * WIDTH * 1024 * 1024, bytes_accessed=4 << 20, transcendentals=0
        ),
    )(core, part, grads, *blocks)


def arrange_kernel(core_ref, own_ref, other_ref, out_ref):
    half = out_ref.shape[1] // 2
    for ref, core in ((own_ref, core_ref[0]), (other_ref, 1 - core_ref[0])):
        for r in range(4):
            for q in range(4):
                lanes = pl.ds(pl.multiple_of(core * half + q * 128, 128), 128)
                out_ref[r * 72 : (r + 1) * 72, lanes] = ref[4 * r + q]


def arrange(core, own, other):
    return pl.pallas_call(
        arrange_kernel,
        out_shape=jax.ShapeDtypeStruct((WIDTH, D // PARTS), F32),
        in_specs=[SMEM, VMEM, VMEM],
        out_specs=VMEM,
        compiler_params=params(16),
    )(core, own, other)


def swap_all(x, axis, groups=None):
    return lax.all_to_all(x, axis, 0, 0, tiled=True, axis_index_groups=groups)


def spread_hidden(blocks, distances):
    moved = []
    for k in distances:
        route = [(i, (i + k) % PARTS) for i in range(PARTS)]
        moved.append(lax.ppermute(blocks[k], "dp", route))
    return moved


def local(hidden, queries, keys, values, docs, w_proj, conv_weight, dt_bias, decay_rate):
    seq_devices = lax.axis_size("seq")
    data_devices = lax.axis_size("dp")
    seq_len = hidden.shape[1] * seq_devices
    weight = 1.0 / math.sqrt(HEADS * DIM * data_devices * seq_len)
    head = lax.axis_index("seq").astype(jnp.int32)
    core = lax.rem(head, 2)[None]
    part = lax.axis_index("dp").astype(jnp.int32)[None]
    same_core = [[2 * i + c for i in range(seq_devices // 2)] for c in range(2)]
    partner = [(i, i ^ 1) for i in range(seq_devices)]

    turned_w = w_proj.T
    half = turned_w.shape[1] // 2
    own_w = lax.dynamic_slice_in_dim(turned_w, core[0] * half, half, 1)
    own_w = lax.all_gather(own_w, "dp", axis=0)
    own = swap_all(pack_teacher(queries, keys, values, docs), "seq")
    own, own_w, taps, blocks = lax.optimization_barrier(
        (own, own_w, conv_weight.T, pack_hidden(part, hidden))
    )
    order = (4, 5, 3, 6, 2, 1, 7)
    moved = {0: blocks[0]} | dict(zip(order, spread_hidden(blocks, order)))
    other_w = lax.ppermute(own_w, "seq", partner)
    other = lax.ppermute(own[:, ROWS : 2 * ROWS, :], "seq", partner)
    proj = swap_all(project(core, hidden, own_w, other_w), "seq")
    teach, v, vt, counts = attend(core, own, other)
    grads = student(
        head[None], counts, dt_bias, decay_rate, taps, proj, teach, v, vt, weight
    )
    grads, moved = lax.optimization_barrier((grads, moved))
    rounded = swap_all(combine(swap_all(grads, "seq")), "dp")
    keep, send = product(core, part, rounded, [moved[k] for k in range(PARTS)])
    partial = keep + lax.ppermute(send, "seq", partner)
    total = jnp.sum(swap_all(partial, "seq", same_core), axis=0)
    spread = jnp.broadcast_to(total[None], partial.shape)
    own_blocks = swap_all(spread, "seq", same_core)
    other_blocks = lax.ppermute(own_blocks, "seq", partner)
    return arrange(core, own_blocks, other_blocks).T


def solution(mesh):
    placed = (
        P("dp", "seq", None),
        P("dp", "seq", None),
        P("dp", "seq", None),
        P("dp", "seq", None),
        P("dp", "seq"),
        P("dp", None),
        P(),
        P(),
        P(),
    )
    return jax.shard_map(
        local, mesh=mesh, in_specs=placed, out_specs=P("dp", None), check_vma=False
    )
```

```python
import math

import jax
import jax.numpy as jnp
from jax import lax
from jax.experimental import pallas as pl
from jax.experimental.pallas import tpu as pltpu
from jax.sharding import PartitionSpec as P

D = 8192
HEADS = 32
GROUPS = 8
SHARE = 4
DIM = 128
STATE = 16
TAPS = 4
SEQ = 4096
ROWS = 128
BLOCKS = SEQ // ROWS
PARTS = 8
WIDTH = 288
DOC_ROWS = 16
TEACH_ROWS = 2 * ROWS + DOC_ROWS
COLS = 40
SPAN = 256
CHUNKS = SEQ // SPAN
KEYS = 1024
HALF = KEYS // 2
QUERIES = 512
PAD = max(0, KEYS - QUERIES)
UNROLL = 16
PACK_STEPS = 2
PROJECT_STEPS = 2

F32 = jnp.float32
BF16 = jnp.bfloat16
NEG = -1e30
VMEM = pl.BlockSpec(memory_space=pltpu.VMEM)
SMEM = pl.BlockSpec(memory_space=pltpu.SMEM)
ANY = pl.BlockSpec(memory_space=pl.ANY)

NT = (((1,), (1,)), ((), ()))


def params(mib=56):
    return pltpu.CompilerParams(vmem_limit_bytes=mib << 20)


def mm(a, b):
    return jnp.dot(a, b, preferred_element_type=F32)


def mm_nt(a, b):
    return lax.dot_general(a, b, NT, preferred_element_type=F32)


def split(x):
    high = x.astype(BF16)
    return high, (x - high.astype(F32)).astype(BF16)


def doc_start(position, n_ref):
    start = jnp.where(position >= n_ref[0], n_ref[0], 0)
    start = jnp.where(position >= n_ref[1], n_ref[1], start)
    return jnp.where(position >= n_ref[2], n_ref[2], start)


def scalar_start(position, n_ref):
    return doc_start(position, n_ref)


def pack_teacher_kernel(q_ref, k_ref, v_ref, doc_ref, out_ref):
    docs = jnp.broadcast_to(doc_ref[...].astype(F32), (DOC_ROWS, ROWS)).astype(BF16)
    for k in range(q_ref.shape[2] // DIM):
        g = k // SHARE
        out_ref[k, 0:ROWS, :] = q_ref[0, :, k * DIM : (k + 1) * DIM]
        source = k_ref if k % 2 == 0 else v_ref
        out_ref[k, ROWS : 2 * ROWS, :] = source[0, :, g * DIM : (g + 1) * DIM]
        out_ref[k, 2 * ROWS :, :] = docs


def pack_teacher(q, k, v, docs):
    many = GROUPS // PACK_STEPS
    return pl.pallas_call(
        pack_teacher_kernel,
        out_shape=jax.ShapeDtypeStruct((HEADS, TEACH_ROWS, DIM), BF16),
        grid=(PACK_STEPS,),
        in_specs=[
            pl.BlockSpec((1, ROWS, many * SHARE * DIM), lambda g: (0, 0, g)),
            pl.BlockSpec((1, ROWS, many * DIM), lambda g: (0, 0, g)),
            pl.BlockSpec((1, ROWS, many * DIM), lambda g: (0, 0, g)),
            pl.BlockSpec((1, ROWS), lambda g: (0, 0)),
        ],
        out_specs=pl.BlockSpec((many * SHARE, TEACH_ROWS, DIM), lambda g: (g, 0, 0)),
        compiler_params=params(60),
        cost_estimate=pl.CostEstimate(flops=0, bytes_accessed=4 << 20, transcendentals=0),
    )(q, k, v, docs)


def pack_hidden_kernel(part_ref, hid_ref, *out_refs):
    width = out_refs[0].shape[1]
    for k, ref in enumerate(out_refs):
        block = lax.rem(part_ref[0] + k, PARTS)
        ref[...] = hid_ref[0, :, pl.ds(pl.multiple_of(block * width, width), width)]


def pack_hidden(part, hidden):
    block = jax.ShapeDtypeStruct((ROWS, D // PARTS), BF16)
    return pl.pallas_call(
        pack_hidden_kernel,
        out_shape=(block,) * PARTS,
        in_specs=[SMEM, VMEM],
        out_specs=(VMEM,) * PARTS,
        compiler_params=params(60),
        cost_estimate=pl.CostEstimate(flops=0, bytes_accessed=4 << 20, transcendentals=0),
    )(part, hidden)


def project_kernel(core_ref, hid_ref, own_ref, other_ref, out_ref, acc_ref):
    step = pl.program_id(0)
    many, _, half = own_ref.shape
    part = 0.0
    for i in range(many):
        mine = pl.multiple_of((2 * i + core_ref[0]) * half, half)
        theirs = pl.multiple_of((2 * i + 1 - core_ref[0]) * half, half)
        part = part + mm_nt(own_ref[i], hid_ref[0, :, pl.ds(mine, half)])
        part = part + mm_nt(other_ref[i], hid_ref[0, :, pl.ds(theirs, half)])

    @pl.when(step == 0)
    def _():
        acc_ref[...] = part

    @pl.when(step > 0)
    def _():
        acc_ref[...] += part

    @pl.when(step == PROJECT_STEPS - 1)
    def _():
        for h in range(HEADS):
            g = h // SHARE
            out_ref[h, 0:STATE, :] = acc_ref[g * STATE : (g + 1) * STATE]
            out_ref[h, STATE : 2 * STATE, :] = acc_ref[128 + g * STATE : 128 + (g + 1) * STATE]
            out_ref[h, 2 * STATE :, :] = jnp.broadcast_to(
                acc_ref[256 + h : 257 + h], (COLS - 2 * STATE, ROWS)
            )


def project(core, hidden, own, other):
    _, width, half = own.shape
    many = PARTS // PROJECT_STEPS
    return pl.pallas_call(
        project_kernel,
        out_shape=jax.ShapeDtypeStruct((HEADS, COLS, ROWS), F32),
        grid_spec=pltpu.PrefetchScalarGridSpec(
            num_scalar_prefetch=1,
            grid=(PROJECT_STEPS,),
            in_specs=[
                pl.BlockSpec((1, ROWS, many * 2 * half), lambda i, c: (0, 0, i)),
                pl.BlockSpec((many, width, half), lambda i, c: (i, 0, 0)),
                pl.BlockSpec((many, width, half), lambda i, c: (i, 0, 0)),
            ],
            out_specs=pl.BlockSpec((HEADS, COLS, ROWS), lambda i, c: (0, 0, 0)),
            scratch_shapes=[pltpu.VMEM((width, ROWS), F32)],
        ),
        compiler_params=params(24),
        cost_estimate=pl.CostEstimate(
            flops=2 * ROWS * D * 288, bytes_accessed=8 << 20, transcendentals=0
        ),
    )(core, hidden, own, other)


def attend_kernel(
    core_ref,
    own_ref,
    other_ref,
    teach_ref,
    v_ref,
    vt_ref,
    n_ref,
    queries,
    labels,
    keys,
    values,
    turned,
    mixed,
    scores,
    sems,
    out_sems,
):
    first = PAD // ROWS
    key_part = keys.at[pl.ds(first, BLOCKS)]
    docs_in = pltpu.make_async_copy(own_ref.at[:, pl.ds(2 * ROWS, DOC_ROWS)], labels, sems.at[0])
    query_in = pltpu.make_async_copy(own_ref.at[:, pl.ds(0, ROWS)], queries, sems.at[1])
    own_kv = own_ref.at[:, pl.ds(ROWS, ROWS)]
    is_key = core_ref[0] == 0

    @pl.when(is_key)
    def _():
        pltpu.make_async_copy(other_ref, values, sems.at[2]).start()
        pltpu.make_async_copy(own_kv, key_part, sems.at[3]).start()

    @pl.when(jnp.logical_not(is_key))
    def _():
        pltpu.make_async_copy(own_kv, values, sems.at[2]).start()
        pltpu.make_async_copy(other_ref, key_part, sems.at[3]).start()

    docs_in.start()
    query_in.start()
    keys[0:first] = jnp.zeros((first, ROWS, DIM), BF16)
    turned[:, 0:PAD] = jnp.zeros((DIM, PAD), BF16)
    pltpu.make_async_copy(other_ref, values, sems.at[2]).wait()
    v_out = pltpu.make_async_copy(values, v_ref, out_sems.at[0])
    v_out.start()
    for s in range(BLOCKS):
        turned[:, PAD + s * ROWS : PAD + (s + 1) * ROWS] = values[s].T
    vt_out = pltpu.make_async_copy(turned.at[:, pl.ds(PAD, SEQ)], vt_ref, out_sems.at[1])
    vt_out.start()
    docs_in.wait()
    docs = jnp.max(labels[...].astype(F32), axis=1)
    for d in range(3):
        n_ref[d] = jnp.sum((docs < d + 0.5).astype(F32)).astype(jnp.int32)
    n_ref[3] = 0
    query_in.wait()
    pltpu.make_async_copy(other_ref, key_part, sems.at[3]).wait()

    scale = DIM ** (-0.5) * math.log2(math.e)

    def rows(i, carry):
        q0 = i * QUERIES
        many = QUERIES // ROWS
        query = queries[pl.ds(many * i, many)].reshape(QUERIES, DIM)
        first = scalar_start(q0, n_ref)
        last = scalar_start(q0 + QUERIES - 1, n_ref)
        need = q0 + QUERIES - first
        rest = lax.rem(need, KEYS)
        count = need // KEYS + (rest > HALF).astype(jnp.int32)
        ends = ((rest > 0) & (rest <= HALF)).astype(jnp.int32)
        q_at = q0 + lax.broadcasted_iota(jnp.int32, (1, QUERIES), 1)
        start = doc_start(q_at, n_ref)

        def tile(at, size):
            low = q0 + QUERIES - at - size
            return low, low + PAD, pl.ds(pl.multiple_of(at, HALF), size)

        def score(at, size, masked, top):
            low, key_at, rows_at = tile(at, size)
            block = keys[pl.ds(key_at // ROWS, size // ROWS)].reshape(size, DIM)
            s = mm_nt(block, query)
            if masked:
                k_at = low + lax.broadcasted_iota(jnp.int32, (size, QUERIES), 0)
                s = jnp.where((k_at <= q_at) & (k_at >= start), s, NEG)
            scores[rows_at, :] = s
            return jnp.maximum(top, jnp.max(s.reshape(size // 8, 8, QUERIES), axis=0))

        def masked(j, top):
            return score(j * KEYS, KEYS, True, top)

        def plain(j, top):
            return score(j * KEYS, KEYS, False, top)

        def masked_half(j, top):
            return score(count * KEYS, HALF, True, top)

        one = jnp.minimum(count, 1)
        inner = jnp.clip((q0 + QUERIES - last) // KEYS, one, count)
        top = jnp.full((8, QUERIES), NEG, F32)
        top = lax.fori_loop(0, one, masked, top)
        top = lax.fori_loop(one, inner, plain, top)
        top = lax.fori_loop(inner, count, masked, top)
        top = lax.fori_loop(0, ends, masked_half, top)
        top = jnp.max(top, axis=0, keepdims=True)

        def mix(at, size, state):
            total, out = state
            _, key_at, rows_at = tile(at, size)
            p = jnp.exp2((scores[rows_at, :] - top) * scale)
            total = total + jnp.sum(p.reshape(size // 8, 8, QUERIES), axis=0)
            return total, out + mm(
                turned[:, pl.ds(pl.multiple_of(key_at, HALF), size)], p.astype(BF16)
            )

        state = (jnp.zeros((8, QUERIES), F32), jnp.zeros((DIM, QUERIES), F32))
        state = lax.fori_loop(0, count, lambda j, t: mix(j * KEYS, KEYS, t), state)
        total, out = lax.fori_loop(0, ends, lambda j, t: mix(count * KEYS, HALF, t), state)
        total = jnp.sum(total, axis=0, keepdims=True)
        mixed[i] = (out / total).astype(BF16)
        teach_out(i).start()
        return carry

    def teach_out(i):
        lanes = pl.ds(pl.multiple_of(i * QUERIES, QUERIES), QUERIES)
        return pltpu.make_async_copy(mixed.at[i], teach_ref.at[:, lanes], out_sems.at[2 + i])

    lax.fori_loop(0, SEQ // QUERIES, rows, 0)
    v_out.wait()
    vt_out.wait()
    for i in range(SEQ // QUERIES):
        teach_out(i).wait()


def attend(core, own, other):
    many = SEQ // QUERIES
    return pl.pallas_call(
        attend_kernel,
        out_shape=(
            jax.ShapeDtypeStruct((DIM, SEQ), BF16),
            jax.ShapeDtypeStruct((BLOCKS, ROWS, DIM), BF16),
            jax.ShapeDtypeStruct((DIM, SEQ), BF16),
            jax.ShapeDtypeStruct((4,), jnp.int32),
        ),
        in_specs=[SMEM, ANY, ANY],
        out_specs=(ANY, ANY, ANY, SMEM),
        scratch_shapes=[
            pltpu.VMEM((BLOCKS, ROWS, DIM), BF16),
            pltpu.VMEM((BLOCKS, DOC_ROWS, DIM), BF16),
            pltpu.VMEM((BLOCKS + PAD // ROWS, ROWS, DIM), BF16),
            pltpu.VMEM((BLOCKS, ROWS, DIM), BF16),
            pltpu.VMEM((DIM, PAD + SEQ), BF16),
            pltpu.VMEM((many, DIM, QUERIES), BF16),
            pltpu.VMEM((SEQ + KEYS, QUERIES), F32),
            pltpu.SemaphoreType.DMA((4,)),
            pltpu.SemaphoreType.DMA((2 + many,)),
        ],
        compiler_params=params(),
        cost_estimate=pl.CostEstimate(
            flops=8 << 30, bytes_accessed=8 << 20, transcendentals=8 << 20
        ),
    )(core, own, other)


def scan_lanes(x, reverse):
    width = x.shape[1]
    lane = lax.broadcasted_iota(jnp.int32, x.shape, 1)
    step = 1
    while step < width:
        if reverse:
            moved = pltpu.roll(x, width - step, 1)
            x = x + jnp.where(lane < width - step, moved, 0.0)
        else:
            moved = pltpu.roll(x, step, 1)
            x = x + jnp.where(lane >= step, moved, 0.0)
        step *= 2
    return x


def student_kernel(
    head_ref,
    n_ref,
    bias_ref,
    rate_ref,
    taps_ref,
    proj_ref,
    teach_ref,
    v_ref,
    vt_ref,
    out_ref,
    source,
    steps,
    cums,
    columns,
    pre_s,
    sig_s,
    z_s,
    dc_s,
    q_s,
    x_s,
    direct_s,
    state_s,
    dstate_s,
    *,
    weight,
):
    head = head_ref[0]
    group = head // SHARE
    bias = bias_ref[head]
    rate = rate_ref[head]
    lane = lax.broadcasted_iota(jnp.int32, (1, SPAN), 1)
    deep = lax.broadcasted_iota(jnp.int32, (SPAN, SPAN), 0)
    taps_b = taps_ref[pl.ds(pl.multiple_of(group * STATE, STATE), STATE), :]
    taps_c = taps_ref[pl.ds(pl.multiple_of(128 + group * STATE, STATE), STATE), :]
    taps = jnp.concatenate([taps_b, taps_c], 0)

    source[:, 0:128] = jnp.zeros((2 * STATE, 128), F32)
    for s in range(BLOCKS):
        source[:, 128 + s * ROWS : 128 + (s + 1) * ROWS] = proj_ref[s, 0 : 2 * STATE, :]
        steps[s // 2 : s // 2 + 1, (s % 2) * ROWS : (s % 2 + 1) * ROWS] = proj_ref[
            s, 2 * STATE : 2 * STATE + 1, :
        ]
    raw = steps[...] + bias
    step_all = jnp.maximum(raw, 0.0) + jnp.log1p(jnp.exp(-jnp.abs(raw)))
    slope_all = 1.0 / (1.0 + jnp.exp(-raw))
    steps[...] = step_all
    cum_all = scan_lanes(-step_all * rate, False)
    cums[...] = cum_all
    cum_turned = cum_all.T
    for c in range(CHUNKS):
        columns[c] = cum_turned[:, c : c + 1]

    def marks(c):
        base = c * SPAN
        at = base + lane
        start = doc_start(at, n_ref)
        last = scalar_start(base + SPAN - 1, n_ref)
        return base, at, start, last

    def forward(c, state):
        base, at, start, last = marks(c)
        wide = pl.multiple_of(base, SPAN)
        rows = source[:, pl.ds(wide, SPAN + 128)]
        pre = taps[:, 0:1] * rows[:, 128:]
        for j in range(1, TAPS):
            lagged = jnp.where(at - j >= start, pltpu.roll(rows, j, 1)[:, 128:], 0.0)
            pre = pre + taps[:, j : j + 1] * lagged
        sig = 1.0 / (1.0 + jnp.exp(-pre))
        gates = pre * sig
        pre_s[:, pl.ds(wide, SPAN)] = pre
        sig_s[:, pl.ds(wide, SPAN)] = sig
        gate_c = gates[STATE:]
        step = steps[pl.ds(c, 1), :]
        cum = cums[pl.ds(c, 1), :]
        ended = cum[:, SPAN - 1 :]
        fed = gates[:STATE] * step
        fed_high, fed_low = split(fed)
        c_high, c_low = split(gate_c)
        fed_stack = jnp.concatenate([fed, fed_low.astype(F32), fed], 0)
        left = fed_stack.T.astype(BF16)
        inner = mm(left, jnp.concatenate([c_high, c_high, c_low], 0))
        allowed = (deep <= lane) & (deep >= start - base)
        fade = jnp.exp(jnp.where(allowed, cum - columns[c], NEG))
        mixing = fade * inner
        mix_high, mix_low = split(mixing)
        values = v_ref[pl.ds(2 * c, 2)].reshape(SPAN, DIM)
        turned = vt_ref[:, pl.ds(wide, SPAN)]
        enter = jnp.where(start < base, jnp.exp(cum), 0.0)
        entered = gate_c * enter
        in_high, in_low = split(entered)
        s_high, s_low = split(state)
        state_left = jnp.concatenate([state, s_low.astype(F32), state], 0).T.astype(BF16)
        out = mm(turned, mix_high) + mm(turned, mix_low)
        out = out + mm(state_left, jnp.concatenate([in_high, in_high, in_low], 0))
        wanted = teach_ref[:, pl.ds(wide, SPAN)].astype(F32)
        error = (out - wanted) * weight
        q_s[pl.ds(c, 1), :] = jnp.sum(out * error, axis=0, keepdims=True)
        e_high, e_low = split(error)
        e_stack = jnp.concatenate([e_high, e_low], 0)
        pulled = fade * mm(jnp.concatenate([values, values], 1), e_stack)
        h_high, h_low = split(pulled)
        c_stack = jnp.concatenate([c_high, c_low], 0)
        z = mm_nt(c_stack, h_high) + mm_nt(c_stack, h_low)
        z_s[:, pl.ds(wide, SPAN)] = z[:STATE] + z[STATE:]
        fed_pair = jnp.concatenate([fed_high, fed_low], 0)
        dc = mm(fed_pair, h_high) + mm(fed_pair, h_low)
        s_pair = jnp.concatenate([s_high, s_low], 0)
        dc_in = mm(s_pair, e_high) + mm(s_pair, e_low)
        dc_s[:, pl.ds(wide, SPAN)] = dc[:STATE] + dc[STATE:] + enter * (dc_in[:STATE] + dc_in[STATE:])
        in_pair = jnp.concatenate([in_high, in_low], 0)
        ds = mm_nt(in_pair, e_high) + mm_nt(in_pair, e_low)
        dstate_s[c] = ds[:STATE] + ds[STATE:]
        state_s[c] = state
        tail = jnp.where(at >= last, jnp.exp(ended - cum), 0.0)
        t_high, t_low = split(fed * tail)
        new = mm(jnp.concatenate([t_high, t_low], 0), values)
        keep = jnp.where(last < base, 1.0, 0.0) * jnp.exp(ended)
        return keep * state + new[:STATE] + new[STATE:]

    final = lax.fori_loop(0, CHUNKS, forward, jnp.zeros((STATE, DIM), F32), unroll=UNROLL)
    state_s[CHUNKS] = final

    def backward(k, carried):
        dstate, later = carried
        c = CHUNKS - 1 - k
        base, at, start, last = marks(c)
        wide = pl.multiple_of(base, SPAN)
        step = steps[pl.ds(c, 1), :]
        cum = cums[pl.ds(c, 1), :]
        ended = cum[:, SPAN - 1 :]
        tail = jnp.where(at >= last, jnp.exp(ended - cum), 0.0)
        d_high, d_low = split(dstate)
        turned = vt_ref[:, pl.ds(wide, SPAN)]
        through = mm(jnp.concatenate([d_high, d_low], 0), turned)
        z = z_s[:, pl.ds(wide, SPAN)] + tail * (through[:STATE] + through[STATE:])
        pre = pre_s[:, pl.ds(wide, SPAN)]
        sig = sig_s[:, pl.ds(wide, SPAN)]
        gates = pre * sig
        direct = jnp.sum(gates[:STATE] * z, axis=0, keepdims=True)
        direct_s[pl.ds(c, 1), :] = direct
        crossing = jnp.sum(jnp.sum(dstate * state_s[c + 1], axis=0, keepdims=True), axis=1, keepdims=True)
        x_s[pl.ds(c, 1), :] = jnp.broadcast_to(crossing, (1, SPAN))
        dgates = jnp.concatenate([step * z, dc_s[:, pl.ds(wide, SPAN)]], 0)
        dpre = dgates * (sig + gates * (1.0 - sig))
        rows = jnp.concatenate([dpre, later], 1)
        back = taps[:, 0:1] * rows[:, :SPAN]
        for j in range(1, TAPS):
            reach = jnp.where(at >= doc_start(at + j, n_ref), pltpu.roll(rows, SPAN + 128 - j, 1)[:, :SPAN], 0.0)
            back = back + taps[:, j : j + 1] * reach
        out_ref[2 * c, 0 : 2 * STATE, :] = back[:, :ROWS]
        out_ref[2 * c + 1, 0 : 2 * STATE, :] = back[:, ROWS:]
        keep = jnp.where(last < base, 1.0, 0.0) * jnp.exp(ended)
        return keep * dstate + dstate_s[c], dpre[:, :128]

    nothing = (jnp.zeros((STATE, DIM), F32), jnp.zeros((2 * STATE, 128), F32))
    lax.fori_loop(0, CHUNKS, backward, nothing, unroll=UNROLL)

    at_all = lax.broadcasted_iota(jnp.int32, (CHUNKS, SPAN), 0) * SPAN
    at_all = at_all + lax.broadcasted_iota(jnp.int32, (CHUNKS, SPAN), 1)
    direct = direct_s[...]
    dlog = scan_lanes(q_s[...] - step_all * direct, True) + x_s[...]
    dlog = jnp.where(at_all > doc_start(at_all, n_ref), dlog, 0.0)
    dstep = (direct - rate * dlog) * slope_all
    for s in range(BLOCKS):
        piece = dstep[s // 2 : s // 2 + 1, (s % 2) * ROWS : (s % 2 + 1) * ROWS]
        out_ref[s, 2 * STATE :, :] = jnp.broadcast_to(piece, (COLS - 2 * STATE, ROWS))


def student(head, counts, bias, rate, taps, proj, teach, v, vt, weight):
    return pl.pallas_call(
        lambda *refs: student_kernel(*refs, weight=weight),
        out_shape=jax.ShapeDtypeStruct((BLOCKS, COLS, ROWS), F32),
        in_specs=[SMEM, SMEM, SMEM, SMEM, VMEM, VMEM, VMEM, VMEM, VMEM],
        out_specs=VMEM,
        scratch_shapes=[
            pltpu.VMEM((2 * STATE, 128 + SEQ), F32),
            pltpu.VMEM((CHUNKS, SPAN), F32),
            pltpu.VMEM((CHUNKS, SPAN), F32),
            pltpu.VMEM((CHUNKS, SPAN, 1), F32),
            pltpu.VMEM((2 * STATE, SEQ), F32),
            pltpu.VMEM((2 * STATE, SEQ), F32),
            pltpu.VMEM((STATE, SEQ), F32),
            pltpu.VMEM((STATE, SEQ), F32),
            pltpu.VMEM((CHUNKS, SPAN), F32),
            pltpu.VMEM((CHUNKS, SPAN), F32),
            pltpu.VMEM((CHUNKS, SPAN), F32),
            pltpu.VMEM((CHUNKS + 1, STATE, DIM), F32),
            pltpu.VMEM((CHUNKS, STATE, DIM), F32),
        ],
        compiler_params=params(56),
        cost_estimate=pl.CostEstimate(
            flops=8 << 30, bytes_accessed=8 << 20, transcendentals=4 << 20
        ),
    )(head, counts, bias, rate, taps, proj, teach, v, vt)


def combine_kernel(in_ref, out_ref, rows):
    for g in range(GROUPS):
        gates = in_ref[SHARE * g, : 2 * STATE]
        for k in range(1, SHARE):
            gates = gates + in_ref[SHARE * g + k, : 2 * STATE]
        rows[g * STATE : (g + 1) * STATE] = gates[:STATE]
        rows[128 + g * STATE : 128 + (g + 1) * STATE] = gates[STATE:]
    for h in range(HEADS):
        rows[256 + h : 257 + h] = in_ref[h, 2 * STATE : 2 * STATE + 1]
    out_ref[...] = rows[...].astype(BF16)


def combine(parts):
    return pl.pallas_call(
        combine_kernel,
        out_shape=jax.ShapeDtypeStruct((WIDTH, ROWS), BF16),
        in_specs=[VMEM],
        out_specs=VMEM,
        scratch_shapes=[pltpu.VMEM((WIDTH, ROWS), F32)],
        compiler_params=params(16),
    )(parts)


def product_kernel(core_ref, *refs):
    grads, blocks, (keep_ref, send_ref) = refs[:PARTS], refs[PARTS : 2 * PARTS], refs[2 * PARTS :]
    left = jnp.concatenate([grad[...] for grad in grads], 1)
    half = blocks[0].shape[1] // 2
    for ref, core in ((send_ref, 1 - core_ref[0]), (keep_ref, core_ref[0])):
        lanes = pl.ds(pl.multiple_of(core * half, half), half)
        part = mm(left, jnp.concatenate([block[:, lanes] for block in blocks], 0))
        for r in range(4):
            for q in range(4):
                ref[4 * r + q] = part[r * 72 : (r + 1) * 72, q * 128 : (q + 1) * 128]


def product(core, grads, blocks):
    shape = jax.ShapeDtypeStruct((16, WIDTH // 4, 128), F32)
    return pl.pallas_call(
        product_kernel,
        out_shape=(shape, shape),
        in_specs=[SMEM] + [VMEM] * (2 * PARTS),
        out_specs=(VMEM, VMEM),
        compiler_params=params(24),
        cost_estimate=pl.CostEstimate(
            flops=2 * WIDTH * 1024 * 1024, bytes_accessed=4 << 20, transcendentals=0
        ),
    )(core, *grads, *blocks)


def arrange_kernel(core_ref, own_ref, other_ref, out_ref):
    half = out_ref.shape[1] // 2
    for ref, core in ((own_ref, core_ref[0]), (other_ref, 1 - core_ref[0])):
        for r in range(4):
            for q in range(4):
                lanes = pl.ds(pl.multiple_of(core * half + q * 128, 128), 128)
                out_ref[r * 72 : (r + 1) * 72, lanes] = ref[4 * r + q]


def arrange(core, own, other):
    return pl.pallas_call(
        arrange_kernel,
        out_shape=jax.ShapeDtypeStruct((WIDTH, D // PARTS), F32),
        in_specs=[SMEM, VMEM, VMEM],
        out_specs=VMEM,
        compiler_params=params(16),
    )(core, own, other)


def swap_all(x, axis, groups=None):
    return lax.all_to_all(x, axis, 0, 0, tiled=True, axis_index_groups=groups)


def spread_hidden(blocks, distances):
    moved = []
    for k in distances:
        route = [(i, (i + k) % PARTS) for i in range(PARTS)]
        moved.append(lax.ppermute(blocks[k], "dp", route))
    return moved


def local(hidden, queries, keys, values, docs, w_proj, conv_weight, dt_bias, decay_rate):
    seq_devices = lax.axis_size("seq")
    data_devices = lax.axis_size("dp")
    seq_len = hidden.shape[1] * seq_devices
    weight = 1.0 / math.sqrt(HEADS * DIM * data_devices * seq_len)
    head = lax.axis_index("seq").astype(jnp.int32)
    core = lax.rem(head, 2)[None]
    part = lax.axis_index("dp").astype(jnp.int32)[None]
    same_core = [[2 * i + c for i in range(seq_devices // 2)] for c in range(2)]
    partner = [(i, i ^ 1) for i in range(seq_devices)]

    turned_w = w_proj.T
    half = turned_w.shape[1] // 2
    own_w = lax.dynamic_slice_in_dim(turned_w, core[0] * half, half, 1)
    own_w = lax.all_gather(own_w, "dp", axis=0)
    own = swap_all(pack_teacher(queries, keys, values, docs), "seq")
    other = lax.ppermute(own[:, ROWS : 2 * ROWS, :], "seq", partner)
    own, other, own_w, taps, blocks = lax.optimization_barrier(
        (own, other, own_w, conv_weight.T, pack_hidden(part, hidden))
    )
    order, last = (4, 5, 3, 6, 2), (1, 7)
    moved = {0: blocks[0]} | dict(zip(order, spread_hidden(blocks, order)))
    waiting = {k: blocks[k] for k in last}
    other_w = lax.ppermute(own_w, "seq", partner)
    proj = swap_all(project(core, hidden, own_w, other_w), "seq")
    teach, v, vt, counts = attend(core, own, other)
    grads = student(
        head[None], counts, dt_bias, decay_rate, taps, proj, teach, v, vt, weight
    )
    grads, moved, waiting = lax.optimization_barrier((grads, moved, waiting))
    rounded, nearby = lax.optimization_barrier(
        (combine(swap_all(grads, "seq")), spread_hidden(waiting, last))
    )
    moved.update(zip(last, nearby))
    far_first = (4, 5, 3, 6, 2, 7, 1)
    copies = {k: rounded for k in far_first}
    spread_grads = {0: rounded} | dict(zip(far_first, spread_hidden(copies, far_first)))
    keep, send = product(
        core, [spread_grads[k] for k in range(PARTS)], [moved[k] for k in range(PARTS)]
    )
    partial = keep + lax.ppermute(send, "seq", partner)
    total = jnp.sum(swap_all(partial, "seq", same_core), axis=0)
    spread = jnp.broadcast_to(total[None], partial.shape)
    own_blocks = swap_all(spread, "seq", same_core)
    other_blocks = lax.ppermute(own_blocks, "seq", partner)
    return arrange(core, own_blocks, other_blocks).T


def solution(mesh):
    placed = (
        P("dp", "seq", None),
        P("dp", "seq", None),
        P("dp", "seq", None),
        P("dp", "seq", None),
        P("dp", "seq"),
        P("dp", None),
        P(),
        P(),
        P(),
    )
    return jax.shard_map(
        local, mesh=mesh, in_specs=placed, out_specs=P("dp", None), check_vma=False
    )
```

```python
import math

import jax
import jax.numpy as jnp
from jax import lax
from jax.experimental import pallas as pl
from jax.experimental.pallas import tpu as pltpu
from jax.sharding import PartitionSpec as P

D = 8192
HEADS = 32
GROUPS = 8
SHARE = 4
DIM = 128
STATE = 16
TAPS = 4
SEQ = 4096
ROWS = 128
BLOCKS = SEQ // ROWS
PARTS = 8
WIDTH = 288
DOC_ROWS = 16
TEACH_ROWS = 2 * ROWS + DOC_ROWS
COLS = 40
SPAN = 256
CHUNKS = SEQ // SPAN
KEYS = 1024
HALF = KEYS // 2
QUERIES = 512
PAD = max(0, KEYS - QUERIES)
UNROLL = 16
PACK_STEPS = 2
PROJECT_STEPS = 2

F32 = jnp.float32
BF16 = jnp.bfloat16
NEG = -1e30
VMEM = pl.BlockSpec(memory_space=pltpu.VMEM)
SMEM = pl.BlockSpec(memory_space=pltpu.SMEM)
ANY = pl.BlockSpec(memory_space=pl.ANY)

NT = (((1,), (1,)), ((), ()))


def params(mib=56):
    return pltpu.CompilerParams(vmem_limit_bytes=mib << 20)


def mm(a, b):
    return jnp.dot(a, b, preferred_element_type=F32)


def mm_nt(a, b):
    return lax.dot_general(a, b, NT, preferred_element_type=F32)


def split(x):
    high = x.astype(BF16)
    return high, (x - high.astype(F32)).astype(BF16)


def doc_start(position, n_ref):
    start = jnp.where(position >= n_ref[0], n_ref[0], 0)
    start = jnp.where(position >= n_ref[1], n_ref[1], start)
    return jnp.where(position >= n_ref[2], n_ref[2], start)


def scalar_start(position, n_ref):
    return doc_start(position, n_ref)


def pack_teacher_kernel(q_ref, k_ref, v_ref, doc_ref, out_ref):
    docs = jnp.broadcast_to(doc_ref[...].astype(F32), (DOC_ROWS, ROWS)).astype(BF16)
    for k in range(q_ref.shape[2] // DIM):
        g = k // SHARE
        out_ref[k, 0:ROWS, :] = q_ref[0, :, k * DIM : (k + 1) * DIM]
        source = k_ref if k % 2 == 0 else v_ref
        out_ref[k, ROWS : 2 * ROWS, :] = source[0, :, g * DIM : (g + 1) * DIM]
        out_ref[k, 2 * ROWS :, :] = docs


def pack_teacher(q, k, v, docs):
    many = GROUPS // PACK_STEPS
    return pl.pallas_call(
        pack_teacher_kernel,
        out_shape=jax.ShapeDtypeStruct((HEADS, TEACH_ROWS, DIM), BF16),
        grid=(PACK_STEPS,),
        in_specs=[
            pl.BlockSpec((1, ROWS, many * SHARE * DIM), lambda g: (0, 0, g)),
            pl.BlockSpec((1, ROWS, many * DIM), lambda g: (0, 0, g)),
            pl.BlockSpec((1, ROWS, many * DIM), lambda g: (0, 0, g)),
            pl.BlockSpec((1, ROWS), lambda g: (0, 0)),
        ],
        out_specs=pl.BlockSpec((many * SHARE, TEACH_ROWS, DIM), lambda g: (g, 0, 0)),
        compiler_params=params(60),
        cost_estimate=pl.CostEstimate(flops=0, bytes_accessed=4 << 20, transcendentals=0),
    )(q, k, v, docs)


def pack_hidden_kernel(core_ref, part_ref, hid_ref, stay_ref, across_ref, mine_ref, give_ref):
    width = stay_ref.shape[1]
    sign = 1 - 2 * core_ref[0]

    def block(distance):
        at = lax.rem(part_ref[0] + distance + PARTS, PARTS)
        return hid_ref[0, :, pl.ds(pl.multiple_of(at * width, width), width)]

    stay_ref[...] = block(0)
    across_ref[...] = block(PARTS // 2)
    for k in range(1, PARTS // 2):
        mine_ref[k - 1] = block(sign * k)
        give_ref[k - 1] = block(-sign * k)


def pack_hidden(core, part, hidden):
    one = jax.ShapeDtypeStruct((ROWS, D // PARTS), BF16)
    three = jax.ShapeDtypeStruct((PARTS // 2 - 1, ROWS, D // PARTS), BF16)
    return pl.pallas_call(
        pack_hidden_kernel,
        out_shape=(one, one, three, three),
        in_specs=[SMEM, SMEM, VMEM],
        out_specs=(VMEM,) * 4,
        compiler_params=params(60),
        cost_estimate=pl.CostEstimate(flops=0, bytes_accessed=4 << 20, transcendentals=0),
    )(core, part, hidden)


def project_kernel(core_ref, hid_ref, own_ref, other_ref, out_ref, acc_ref):
    step = pl.program_id(0)
    many, _, half = own_ref.shape
    part = 0.0
    for i in range(many):
        mine = pl.multiple_of((2 * i + core_ref[0]) * half, half)
        theirs = pl.multiple_of((2 * i + 1 - core_ref[0]) * half, half)
        part = part + mm_nt(own_ref[i], hid_ref[0, :, pl.ds(mine, half)])
        part = part + mm_nt(other_ref[i], hid_ref[0, :, pl.ds(theirs, half)])

    @pl.when(step == 0)
    def _():
        acc_ref[...] = part

    @pl.when(step > 0)
    def _():
        acc_ref[...] += part

    @pl.when(step == PROJECT_STEPS - 1)
    def _():
        for h in range(HEADS):
            g = h // SHARE
            out_ref[h, 0:STATE, :] = acc_ref[g * STATE : (g + 1) * STATE]
            out_ref[h, STATE : 2 * STATE, :] = acc_ref[128 + g * STATE : 128 + (g + 1) * STATE]
            out_ref[h, 2 * STATE :, :] = jnp.broadcast_to(
                acc_ref[256 + h : 257 + h], (COLS - 2 * STATE, ROWS)
            )


def project(core, hidden, own, other):
    _, width, half = own.shape
    many = PARTS // PROJECT_STEPS
    return pl.pallas_call(
        project_kernel,
        out_shape=jax.ShapeDtypeStruct((HEADS, COLS, ROWS), F32),
        grid_spec=pltpu.PrefetchScalarGridSpec(
            num_scalar_prefetch=1,
            grid=(PROJECT_STEPS,),
            in_specs=[
                pl.BlockSpec((1, ROWS, many * 2 * half), lambda i, c: (0, 0, i)),
                pl.BlockSpec((many, width, half), lambda i, c: (i, 0, 0)),
                pl.BlockSpec((many, width, half), lambda i, c: (i, 0, 0)),
            ],
            out_specs=pl.BlockSpec((HEADS, COLS, ROWS), lambda i, c: (0, 0, 0)),
            scratch_shapes=[pltpu.VMEM((width, ROWS), F32)],
        ),
        compiler_params=params(24),
        cost_estimate=pl.CostEstimate(
            flops=2 * ROWS * D * 288, bytes_accessed=8 << 20, transcendentals=0
        ),
    )(core, hidden, own, other)


def attend_kernel(
    core_ref,
    own_ref,
    other_ref,
    teach_ref,
    v_ref,
    vt_ref,
    n_ref,
    queries,
    labels,
    keys,
    values,
    turned,
    mixed,
    scores,
    sems,
    out_sems,
):
    first = PAD // ROWS
    key_part = keys.at[pl.ds(first, BLOCKS)]
    docs_in = pltpu.make_async_copy(own_ref.at[:, pl.ds(2 * ROWS, DOC_ROWS)], labels, sems.at[0])
    query_in = pltpu.make_async_copy(own_ref.at[:, pl.ds(0, ROWS)], queries, sems.at[1])
    own_kv = own_ref.at[:, pl.ds(ROWS, ROWS)]
    is_key = core_ref[0] == 0

    @pl.when(is_key)
    def _():
        pltpu.make_async_copy(other_ref, values, sems.at[2]).start()
        pltpu.make_async_copy(own_kv, key_part, sems.at[3]).start()

    @pl.when(jnp.logical_not(is_key))
    def _():
        pltpu.make_async_copy(own_kv, values, sems.at[2]).start()
        pltpu.make_async_copy(other_ref, key_part, sems.at[3]).start()

    docs_in.start()
    query_in.start()
    keys[0:first] = jnp.zeros((first, ROWS, DIM), BF16)
    turned[:, 0:PAD] = jnp.zeros((DIM, PAD), BF16)
    pltpu.make_async_copy(other_ref, values, sems.at[2]).wait()
    v_out = pltpu.make_async_copy(values, v_ref, out_sems.at[0])
    v_out.start()
    for s in range(BLOCKS):
        turned[:, PAD + s * ROWS : PAD + (s + 1) * ROWS] = values[s].T
    vt_out = pltpu.make_async_copy(turned.at[:, pl.ds(PAD, SEQ)], vt_ref, out_sems.at[1])
    vt_out.start()
    docs_in.wait()
    docs = jnp.max(labels[...].astype(F32), axis=1)
    for d in range(3):
        n_ref[d] = jnp.sum((docs < d + 0.5).astype(F32)).astype(jnp.int32)
    n_ref[3] = 0
    query_in.wait()
    pltpu.make_async_copy(other_ref, key_part, sems.at[3]).wait()

    scale = DIM ** (-0.5) * math.log2(math.e)

    def rows(i, carry):
        q0 = i * QUERIES
        many = QUERIES // ROWS
        query = queries[pl.ds(many * i, many)].reshape(QUERIES, DIM)
        first = scalar_start(q0, n_ref)
        last = scalar_start(q0 + QUERIES - 1, n_ref)
        need = q0 + QUERIES - first
        rest = lax.rem(need, KEYS)
        count = need // KEYS + (rest > HALF).astype(jnp.int32)
        ends = ((rest > 0) & (rest <= HALF)).astype(jnp.int32)
        q_at = q0 + lax.broadcasted_iota(jnp.int32, (1, QUERIES), 1)
        start = doc_start(q_at, n_ref)

        def tile(at, size):
            low = q0 + QUERIES - at - size
            return low, low + PAD, pl.ds(pl.multiple_of(at, HALF), size)

        def score(at, size, masked, top):
            low, key_at, rows_at = tile(at, size)
            block = keys[pl.ds(key_at // ROWS, size // ROWS)].reshape(size, DIM)
            s = mm_nt(block, query)
            if masked:
                k_at = low + lax.broadcasted_iota(jnp.int32, (size, QUERIES), 0)
                s = jnp.where((k_at <= q_at) & (k_at >= start), s, NEG)
            scores[rows_at, :] = s
            return jnp.maximum(top, jnp.max(s.reshape(size // 8, 8, QUERIES), axis=0))

        def masked(j, top):
            return score(j * KEYS, KEYS, True, top)

        def plain(j, top):
            return score(j * KEYS, KEYS, False, top)

        def masked_half(j, top):
            return score(count * KEYS, HALF, True, top)

        one = jnp.minimum(count, 1)
        inner = jnp.clip((q0 + QUERIES - last) // KEYS, one, count)
        top = jnp.full((8, QUERIES), NEG, F32)
        top = lax.fori_loop(0, one, masked, top)
        top = lax.fori_loop(one, inner, plain, top)
        top = lax.fori_loop(inner, count, masked, top)
        top = lax.fori_loop(0, ends, masked_half, top)
        top = jnp.max(top, axis=0, keepdims=True)

        def mix(at, size, state):
            total, out = state
            _, key_at, rows_at = tile(at, size)
            p = jnp.exp2((scores[rows_at, :] - top) * scale)
            total = total + jnp.sum(p.reshape(size // 8, 8, QUERIES), axis=0)
            return total, out + mm(
                turned[:, pl.ds(pl.multiple_of(key_at, HALF), size)], p.astype(BF16)
            )

        state = (jnp.zeros((8, QUERIES), F32), jnp.zeros((DIM, QUERIES), F32))
        state = lax.fori_loop(0, count, lambda j, t: mix(j * KEYS, KEYS, t), state)
        total, out = lax.fori_loop(0, ends, lambda j, t: mix(count * KEYS, HALF, t), state)
        total = jnp.sum(total, axis=0, keepdims=True)
        mixed[i] = (out / total).astype(BF16)
        teach_out(i).start()
        return carry

    def teach_out(i):
        lanes = pl.ds(pl.multiple_of(i * QUERIES, QUERIES), QUERIES)
        return pltpu.make_async_copy(mixed.at[i], teach_ref.at[:, lanes], out_sems.at[2 + i])

    lax.fori_loop(0, SEQ // QUERIES, rows, 0)
    v_out.wait()
    vt_out.wait()
    for i in range(SEQ // QUERIES):
        teach_out(i).wait()


def attend(core, own, other):
    many = SEQ // QUERIES
    return pl.pallas_call(
        attend_kernel,
        out_shape=(
            jax.ShapeDtypeStruct((DIM, SEQ), BF16),
            jax.ShapeDtypeStruct((BLOCKS, ROWS, DIM), BF16),
            jax.ShapeDtypeStruct((DIM, SEQ), BF16),
            jax.ShapeDtypeStruct((4,), jnp.int32),
        ),
        in_specs=[SMEM, ANY, ANY],
        out_specs=(ANY, ANY, ANY, SMEM),
        scratch_shapes=[
            pltpu.VMEM((BLOCKS, ROWS, DIM), BF16),
            pltpu.VMEM((BLOCKS, DOC_ROWS, DIM), BF16),
            pltpu.VMEM((BLOCKS + PAD // ROWS, ROWS, DIM), BF16),
            pltpu.VMEM((BLOCKS, ROWS, DIM), BF16),
            pltpu.VMEM((DIM, PAD + SEQ), BF16),
            pltpu.VMEM((many, DIM, QUERIES), BF16),
            pltpu.VMEM((SEQ + KEYS, QUERIES), F32),
            pltpu.SemaphoreType.DMA((4,)),
            pltpu.SemaphoreType.DMA((2 + many,)),
        ],
        compiler_params=params(),
        cost_estimate=pl.CostEstimate(
            flops=8 << 30, bytes_accessed=8 << 20, transcendentals=8 << 20
        ),
    )(core, own, other)


def scan_lanes(x, reverse):
    width = x.shape[1]
    lane = lax.broadcasted_iota(jnp.int32, x.shape, 1)
    step = 1
    while step < width:
        if reverse:
            moved = pltpu.roll(x, width - step, 1)
            x = x + jnp.where(lane < width - step, moved, 0.0)
        else:
            moved = pltpu.roll(x, step, 1)
            x = x + jnp.where(lane >= step, moved, 0.0)
        step *= 2
    return x


def student_kernel(
    head_ref,
    n_ref,
    bias_ref,
    rate_ref,
    taps_ref,
    proj_ref,
    teach_ref,
    v_ref,
    vt_ref,
    out_ref,
    source,
    steps,
    cums,
    columns,
    pre_s,
    sig_s,
    z_s,
    dc_s,
    q_s,
    x_s,
    direct_s,
    state_s,
    dstate_s,
    *,
    weight,
):
    head = head_ref[0]
    group = head // SHARE
    bias = bias_ref[head]
    rate = rate_ref[head]
    lane = lax.broadcasted_iota(jnp.int32, (1, SPAN), 1)
    deep = lax.broadcasted_iota(jnp.int32, (SPAN, SPAN), 0)
    taps_b = taps_ref[pl.ds(pl.multiple_of(group * STATE, STATE), STATE), :]
    taps_c = taps_ref[pl.ds(pl.multiple_of(128 + group * STATE, STATE), STATE), :]
    taps = jnp.concatenate([taps_b, taps_c], 0)

    source[:, 0:128] = jnp.zeros((2 * STATE, 128), F32)
    for s in range(BLOCKS):
        source[:, 128 + s * ROWS : 128 + (s + 1) * ROWS] = proj_ref[s, 0 : 2 * STATE, :]
        steps[s // 2 : s // 2 + 1, (s % 2) * ROWS : (s % 2 + 1) * ROWS] = proj_ref[
            s, 2 * STATE : 2 * STATE + 1, :
        ]
    raw = steps[...] + bias
    step_all = jnp.maximum(raw, 0.0) + jnp.log1p(jnp.exp(-jnp.abs(raw)))
    slope_all = 1.0 / (1.0 + jnp.exp(-raw))
    steps[...] = step_all
    cum_all = scan_lanes(-step_all * rate, False)
    cums[...] = cum_all
    cum_turned = cum_all.T
    for c in range(CHUNKS):
        columns[c] = cum_turned[:, c : c + 1]

    def marks(c):
        base = c * SPAN
        at = base + lane
        start = doc_start(at, n_ref)
        last = scalar_start(base + SPAN - 1, n_ref)
        return base, at, start, last

    def forward(c, state):
        base, at, start, last = marks(c)
        wide = pl.multiple_of(base, SPAN)
        rows = source[:, pl.ds(wide, SPAN + 128)]
        pre = taps[:, 0:1] * rows[:, 128:]
        for j in range(1, TAPS):
            lagged = jnp.where(at - j >= start, pltpu.roll(rows, j, 1)[:, 128:], 0.0)
            pre = pre + taps[:, j : j + 1] * lagged
        sig = 1.0 / (1.0 + jnp.exp(-pre))
        gates = pre * sig
        pre_s[:, pl.ds(wide, SPAN)] = pre
        sig_s[:, pl.ds(wide, SPAN)] = sig
        gate_c = gates[STATE:]
        step = steps[pl.ds(c, 1), :]
        cum = cums[pl.ds(c, 1), :]
        ended = cum[:, SPAN - 1 :]
        fed = gates[:STATE] * step
        fed_high, fed_low = split(fed)
        c_high, c_low = split(gate_c)
        fed_stack = jnp.concatenate([fed, fed_low.astype(F32), fed], 0)
        left = fed_stack.T.astype(BF16)
        inner = mm(left, jnp.concatenate([c_high, c_high, c_low], 0))
        allowed = (deep <= lane) & (deep >= start - base)
        fade = jnp.exp(jnp.where(allowed, cum - columns[c], NEG))
        mixing = fade * inner
        mix_high, mix_low = split(mixing)
        values = v_ref[pl.ds(2 * c, 2)].reshape(SPAN, DIM)
        turned = vt_ref[:, pl.ds(wide, SPAN)]
        enter = jnp.where(start < base, jnp.exp(cum), 0.0)
        entered = gate_c * enter
        in_high, in_low = split(entered)
        s_high, s_low = split(state)
        state_left = jnp.concatenate([state, s_low.astype(F32), state], 0).T.astype(BF16)
        out = mm(turned, mix_high) + mm(turned, mix_low)
        out = out + mm(state_left, jnp.concatenate([in_high, in_high, in_low], 0))
        wanted = teach_ref[:, pl.ds(wide, SPAN)].astype(F32)
        error = (out - wanted) * weight
        q_s[pl.ds(c, 1), :] = jnp.sum(out * error, axis=0, keepdims=True)
        e_high, e_low = split(error)
        e_stack = jnp.concatenate([e_high, e_low], 0)
        pulled = fade * mm(jnp.concatenate([values, values], 1), e_stack)
        h_high, h_low = split(pulled)
        c_stack = jnp.concatenate([c_high, c_low], 0)
        z = mm_nt(c_stack, h_high) + mm_nt(c_stack, h_low)
        z_s[:, pl.ds(wide, SPAN)] = z[:STATE] + z[STATE:]
        fed_pair = jnp.concatenate([fed_high, fed_low], 0)
        dc = mm(fed_pair, h_high) + mm(fed_pair, h_low)
        s_pair = jnp.concatenate([s_high, s_low], 0)
        dc_in = mm(s_pair, e_high) + mm(s_pair, e_low)
        dc_s[:, pl.ds(wide, SPAN)] = dc[:STATE] + dc[STATE:] + enter * (dc_in[:STATE] + dc_in[STATE:])
        in_pair = jnp.concatenate([in_high, in_low], 0)
        ds = mm_nt(in_pair, e_high) + mm_nt(in_pair, e_low)
        dstate_s[c] = ds[:STATE] + ds[STATE:]
        state_s[c] = state
        tail = jnp.where(at >= last, jnp.exp(ended - cum), 0.0)
        t_high, t_low = split(fed * tail)
        new = mm(jnp.concatenate([t_high, t_low], 0), values)
        keep = jnp.where(last < base, 1.0, 0.0) * jnp.exp(ended)
        return keep * state + new[:STATE] + new[STATE:]

    final = lax.fori_loop(0, CHUNKS, forward, jnp.zeros((STATE, DIM), F32), unroll=UNROLL)
    state_s[CHUNKS] = final

    def backward(k, carried):
        dstate, later = carried
        c = CHUNKS - 1 - k
        base, at, start, last = marks(c)
        wide = pl.multiple_of(base, SPAN)
        step = steps[pl.ds(c, 1), :]
        cum = cums[pl.ds(c, 1), :]
        ended = cum[:, SPAN - 1 :]
        tail = jnp.where(at >= last, jnp.exp(ended - cum), 0.0)
        d_high, d_low = split(dstate)
        turned = vt_ref[:, pl.ds(wide, SPAN)]
        through = mm(jnp.concatenate([d_high, d_low], 0), turned)
        z = z_s[:, pl.ds(wide, SPAN)] + tail * (through[:STATE] + through[STATE:])
        pre = pre_s[:, pl.ds(wide, SPAN)]
        sig = sig_s[:, pl.ds(wide, SPAN)]
        gates = pre * sig
        direct = jnp.sum(gates[:STATE] * z, axis=0, keepdims=True)
        direct_s[pl.ds(c, 1), :] = direct
        crossing = jnp.sum(jnp.sum(dstate * state_s[c + 1], axis=0, keepdims=True), axis=1, keepdims=True)
        x_s[pl.ds(c, 1), :] = jnp.broadcast_to(crossing, (1, SPAN))
        dgates = jnp.concatenate([step * z, dc_s[:, pl.ds(wide, SPAN)]], 0)
        dpre = dgates * (sig + gates * (1.0 - sig))
        rows = jnp.concatenate([dpre, later], 1)
        back = taps[:, 0:1] * rows[:, :SPAN]
        for j in range(1, TAPS):
            reach = jnp.where(at >= doc_start(at + j, n_ref), pltpu.roll(rows, SPAN + 128 - j, 1)[:, :SPAN], 0.0)
            back = back + taps[:, j : j + 1] * reach
        out_ref[2 * c, 0 : 2 * STATE, :] = back[:, :ROWS]
        out_ref[2 * c + 1, 0 : 2 * STATE, :] = back[:, ROWS:]
        keep = jnp.where(last < base, 1.0, 0.0) * jnp.exp(ended)
        return keep * dstate + dstate_s[c], dpre[:, :128]

    nothing = (jnp.zeros((STATE, DIM), F32), jnp.zeros((2 * STATE, 128), F32))
    lax.fori_loop(0, CHUNKS, backward, nothing, unroll=UNROLL)

    at_all = lax.broadcasted_iota(jnp.int32, (CHUNKS, SPAN), 0) * SPAN
    at_all = at_all + lax.broadcasted_iota(jnp.int32, (CHUNKS, SPAN), 1)
    direct = direct_s[...]
    dlog = scan_lanes(q_s[...] - step_all * direct, True) + x_s[...]
    dlog = jnp.where(at_all > doc_start(at_all, n_ref), dlog, 0.0)
    dstep = (direct - rate * dlog) * slope_all
    for s in range(BLOCKS):
        piece = dstep[s // 2 : s // 2 + 1, (s % 2) * ROWS : (s % 2 + 1) * ROWS]
        out_ref[s, 2 * STATE :, :] = jnp.broadcast_to(piece, (COLS - 2 * STATE, ROWS))


def student(head, counts, bias, rate, taps, proj, teach, v, vt, weight):
    return pl.pallas_call(
        lambda *refs: student_kernel(*refs, weight=weight),
        out_shape=jax.ShapeDtypeStruct((BLOCKS, COLS, ROWS), F32),
        in_specs=[SMEM, SMEM, SMEM, SMEM, VMEM, VMEM, VMEM, VMEM, VMEM],
        out_specs=VMEM,
        scratch_shapes=[
            pltpu.VMEM((2 * STATE, 128 + SEQ), F32),
            pltpu.VMEM((CHUNKS, SPAN), F32),
            pltpu.VMEM((CHUNKS, SPAN), F32),
            pltpu.VMEM((CHUNKS, SPAN, 1), F32),
            pltpu.VMEM((2 * STATE, SEQ), F32),
            pltpu.VMEM((2 * STATE, SEQ), F32),
            pltpu.VMEM((STATE, SEQ), F32),
            pltpu.VMEM((STATE, SEQ), F32),
            pltpu.VMEM((CHUNKS, SPAN), F32),
            pltpu.VMEM((CHUNKS, SPAN), F32),
            pltpu.VMEM((CHUNKS, SPAN), F32),
            pltpu.VMEM((CHUNKS + 1, STATE, DIM), F32),
            pltpu.VMEM((CHUNKS, STATE, DIM), F32),
        ],
        compiler_params=params(56),
        cost_estimate=pl.CostEstimate(
            flops=8 << 30, bytes_accessed=8 << 20, transcendentals=4 << 20
        ),
    )(head, counts, bias, rate, taps, proj, teach, v, vt)


def combine_kernel(in_ref, out_ref, rows):
    for g in range(GROUPS):
        gates = in_ref[SHARE * g, : 2 * STATE]
        for k in range(1, SHARE):
            gates = gates + in_ref[SHARE * g + k, : 2 * STATE]
        rows[g * STATE : (g + 1) * STATE] = gates[:STATE]
        rows[128 + g * STATE : 128 + (g + 1) * STATE] = gates[STATE:]
    for h in range(HEADS):
        rows[256 + h : 257 + h] = in_ref[h, 2 * STATE : 2 * STATE + 1]
    out_ref[...] = rows[...].astype(BF16)


def combine(parts):
    return pl.pallas_call(
        combine_kernel,
        out_shape=jax.ShapeDtypeStruct((WIDTH, ROWS), BF16),
        in_specs=[VMEM],
        out_specs=VMEM,
        scratch_shapes=[pltpu.VMEM((WIDTH, ROWS), F32)],
        compiler_params=params(16),
    )(parts)


def product_kernel(core_ref, *refs):
    count = PARTS // 2 + 1
    grads, blocks, (keep_ref, send_ref) = refs[:count], refs[count : 2 * count], refs[2 * count :]
    left = []
    for grad in grads:
        left += [grad[...]] if len(grad.shape) == 2 else [grad[0], grad[1]]
    left = jnp.concatenate(left, 1)
    half = blocks[0].shape[-1] // 2
    for ref, core in ((send_ref, 1 - core_ref[0]), (keep_ref, core_ref[0])):
        lanes = pl.ds(pl.multiple_of(core * half, half), half)
        right = []
        for block in blocks:
            if len(block.shape) == 2:
                right.append(block[:, lanes])
            else:
                right += [block[0, :, lanes], block[1, :, lanes]]
        part = mm(left, jnp.concatenate(right, 0))
        for r in range(4):
            for q in range(4):
                ref[4 * r + q] = part[r * 72 : (r + 1) * 72, q * 128 : (q + 1) * 128]


def product(core, grads, blocks):
    shape = jax.ShapeDtypeStruct((16, WIDTH // 4, 128), F32)
    return pl.pallas_call(
        product_kernel,
        out_shape=(shape, shape),
        in_specs=[SMEM] + [VMEM] * (PARTS + 2),
        out_specs=(VMEM, VMEM),
        compiler_params=params(24),
        cost_estimate=pl.CostEstimate(
            flops=2 * WIDTH * 1024 * 1024, bytes_accessed=4 << 20, transcendentals=0
        ),
    )(core, *grads, *blocks)


def arrange_kernel(core_ref, own_ref, other_ref, out_ref):
    half = out_ref.shape[1] // 2
    for ref, core in ((own_ref, core_ref[0]), (other_ref, 1 - core_ref[0])):
        for r in range(4):
            for q in range(4):
                lanes = pl.ds(pl.multiple_of(core * half + q * 128, 128), 128)
                out_ref[r * 72 : (r + 1) * 72, lanes] = ref[4 * r + q]


def arrange(core, own, other):
    return pl.pallas_call(
        arrange_kernel,
        out_shape=jax.ShapeDtypeStruct((WIDTH, D // PARTS), F32),
        in_specs=[SMEM, VMEM, VMEM],
        out_specs=VMEM,
        compiler_params=params(16),
    )(core, own, other)


def swap_all(x, axis, groups=None):
    return lax.all_to_all(x, axis, 0, 0, tiled=True, axis_index_groups=groups)


def both_ways(block, distance):
    route = []
    for s in range(lax.axis_size("seq")):
        sign = 1 - 2 * (s % 2)
        for z in range(PARTS):
            route.append((s * PARTS + z, s * PARTS + (z + sign * distance) % PARTS))
    return lax.ppermute(block, ("seq", "dp"), route)


def local(hidden, queries, keys, values, docs, w_proj, conv_weight, dt_bias, decay_rate):
    seq_devices = lax.axis_size("seq")
    data_devices = lax.axis_size("dp")
    seq_len = hidden.shape[1] * seq_devices
    weight = 1.0 / math.sqrt(HEADS * DIM * data_devices * seq_len)
    head = lax.axis_index("seq").astype(jnp.int32)
    core = lax.rem(head, 2)[None]
    part = lax.axis_index("dp").astype(jnp.int32)[None]
    same_core = [[2 * i + c for i in range(seq_devices // 2)] for c in range(2)]
    partner = [(i, i ^ 1) for i in range(seq_devices)]

    turned_w = w_proj.T
    half = turned_w.shape[1] // 2
    own_w = lax.dynamic_slice_in_dim(turned_w, core[0] * half, half, 1)
    own_w = lax.all_gather(own_w, "dp", axis=0)
    own = swap_all(pack_teacher(queries, keys, values, docs), "seq")
    stay, across, mine, give = pack_hidden(core, part, hidden)
    taken = lax.ppermute(give, "seq", partner)
    outgoing = [across] + [jnp.stack([mine[k], taken[k]]) for k in range(PARTS // 2 - 1)]
    own, outgoing, taps = lax.optimization_barrier((own, outgoing, conv_weight.T))
    other = lax.ppermute(own[:, ROWS : 2 * ROWS, :], "seq", partner)
    own, other, own_w, outgoing = lax.optimization_barrier((own, other, own_w, outgoing))
    other_w = lax.ppermute(own_w, "seq", partner)
    far = PARTS // 2
    arrived = {far: both_ways(outgoing[0], far)}
    for k in (3, 2):
        arrived[k] = both_ways(outgoing[k], k)
    late = {k: outgoing[k] for k in (1,)}
    proj = swap_all(project(core, hidden, own_w, other_w), "seq")
    teach, v, vt, counts = attend(core, own, other)
    grads = student(
        head[None], counts, dt_bias, decay_rate, taps, proj, teach, v, vt, weight
    )
    grads, arrived, late = lax.optimization_barrier((grads, arrived, late))
    late = {k: both_ways(late[k], k) for k in late}
    rounded, late = lax.optimization_barrier((combine(swap_all(grads, "seq")), late))
    arrived.update(late)
    spread_grads = {far: both_ways(rounded, far)}
    pair = jnp.stack([rounded, lax.ppermute(rounded, "seq", partner)])
    order = (far, 3, 2, 1)
    for k in order[1:]:
        spread_grads[k] = both_ways(pair, k)
    keep, send = product(
        core,
        [rounded] + [spread_grads[k] for k in order],
        [stay] + [arrived[k] for k in order],
    )
    partial = keep + lax.ppermute(send, "seq", partner)
    total = jnp.sum(swap_all(partial, "seq", same_core), axis=0)
    spread = jnp.broadcast_to(total[None], partial.shape)
    own_blocks = swap_all(spread, "seq", same_core)
    other_blocks = lax.ppermute(own_blocks, "seq", partner)
    return arrange(core, own_blocks, other_blocks).T


def solution(mesh):
    placed = (
        P("dp", "seq", None),
        P("dp", "seq", None),
        P("dp", "seq", None),
        P("dp", "seq", None),
        P("dp", "seq"),
        P("dp", None),
        P(),
        P(),
        P(),
    )
    return jax.shard_map(
        local, mesh=mesh, in_specs=placed, out_specs=P("dp", None), check_vma=False
    )
```

```python
import math

import jax
import jax.numpy as jnp
from jax import lax
from jax.experimental import pallas as pl
from jax.experimental.pallas import tpu as pltpu
from jax.sharding import PartitionSpec as P

D = 8192
HEADS = 32
GROUPS = 8
SHARE = 4
DIM = 128
STATE = 16
TAPS = 4
SEQ = 4096
ROWS = 128
BLOCKS = SEQ // ROWS
PARTS = 8
WIDTH = 288
DOC_ROWS = 16
TEACH_ROWS = 2 * ROWS + DOC_ROWS
COLS = 40
SPAN = 256
CHUNKS = SEQ // SPAN
KEYS = 1024
HALF = KEYS // 2
QUERIES = 512
PAD = max(0, KEYS - QUERIES)
UNROLL = 16
PACK_STEPS = 2
PROJECT_STEPS = 2

F32 = jnp.float32
BF16 = jnp.bfloat16
NEG = -1e30
VMEM = pl.BlockSpec(memory_space=pltpu.VMEM)
SMEM = pl.BlockSpec(memory_space=pltpu.SMEM)
ANY = pl.BlockSpec(memory_space=pl.ANY)

NT = (((1,), (1,)), ((), ()))


def params(mib=56):
    return pltpu.CompilerParams(vmem_limit_bytes=mib << 20)


def mm(a, b):
    return jnp.dot(a, b, preferred_element_type=F32)


def mm_nt(a, b):
    return lax.dot_general(a, b, NT, preferred_element_type=F32)


def split(x):
    high = x.astype(BF16)
    return high, (x - high.astype(F32)).astype(BF16)


def doc_start(position, n_ref):
    start = jnp.where(position >= n_ref[0], n_ref[0], 0)
    start = jnp.where(position >= n_ref[1], n_ref[1], start)
    return jnp.where(position >= n_ref[2], n_ref[2], start)


def scalar_start(position, n_ref):
    return doc_start(position, n_ref)


def pack_teacher_kernel(q_ref, k_ref, v_ref, doc_ref, out_ref):
    docs = jnp.broadcast_to(doc_ref[...].astype(F32), (DOC_ROWS, ROWS)).astype(BF16)
    for k in range(q_ref.shape[2] // DIM):
        g = k // SHARE
        out_ref[k, 0:ROWS, :] = q_ref[0, :, k * DIM : (k + 1) * DIM]
        source = k_ref if k % 2 == 0 else v_ref
        out_ref[k, ROWS : 2 * ROWS, :] = source[0, :, g * DIM : (g + 1) * DIM]
        out_ref[k, 2 * ROWS :, :] = docs


def pack_teacher(q, k, v, docs):
    many = GROUPS // PACK_STEPS
    return pl.pallas_call(
        pack_teacher_kernel,
        out_shape=jax.ShapeDtypeStruct((HEADS, TEACH_ROWS, DIM), BF16),
        grid=(PACK_STEPS,),
        in_specs=[
            pl.BlockSpec((1, ROWS, many * SHARE * DIM), lambda g: (0, 0, g)),
            pl.BlockSpec((1, ROWS, many * DIM), lambda g: (0, 0, g)),
            pl.BlockSpec((1, ROWS, many * DIM), lambda g: (0, 0, g)),
            pl.BlockSpec((1, ROWS), lambda g: (0, 0)),
        ],
        out_specs=pl.BlockSpec((many * SHARE, TEACH_ROWS, DIM), lambda g: (g, 0, 0)),
        compiler_params=params(60),
        cost_estimate=pl.CostEstimate(flops=0, bytes_accessed=4 << 20, transcendentals=0),
    )(q, k, v, docs)


def pack_hidden_kernel(core_ref, part_ref, hid_ref, stay_ref, across_ref, mine_ref, give_ref):
    width = stay_ref.shape[1]
    sign = 1 - 2 * core_ref[0]

    def block(distance):
        at = lax.rem(part_ref[0] + distance + PARTS, PARTS)
        return hid_ref[0, :, pl.ds(pl.multiple_of(at * width, width), width)]

    stay_ref[...] = block(0)
    across_ref[...] = block(PARTS // 2)
    for k in range(1, PARTS // 2):
        mine_ref[k - 1] = block(sign * k)
        give_ref[k - 1] = block(-sign * k)


def pack_hidden(core, part, hidden):
    one = jax.ShapeDtypeStruct((ROWS, D // PARTS), BF16)
    three = jax.ShapeDtypeStruct((PARTS // 2 - 1, ROWS, D // PARTS), BF16)
    return pl.pallas_call(
        pack_hidden_kernel,
        out_shape=(one, one, three, three),
        in_specs=[SMEM, SMEM, VMEM],
        out_specs=(VMEM,) * 4,
        compiler_params=params(60),
        cost_estimate=pl.CostEstimate(flops=0, bytes_accessed=4 << 20, transcendentals=0),
    )(core, part, hidden)


def project_kernel(core_ref, hid_ref, own_ref, other_ref, out_ref, acc_ref):
    step = pl.program_id(0)
    many, _, half = own_ref.shape
    part = 0.0
    for i in range(many):
        mine = pl.multiple_of((2 * i + core_ref[0]) * half, half)
        theirs = pl.multiple_of((2 * i + 1 - core_ref[0]) * half, half)
        part = part + mm_nt(own_ref[i], hid_ref[0, :, pl.ds(mine, half)])
        part = part + mm_nt(other_ref[i], hid_ref[0, :, pl.ds(theirs, half)])

    @pl.when(step == 0)
    def _():
        acc_ref[...] = part

    @pl.when(step > 0)
    def _():
        acc_ref[...] += part

    @pl.when(step == PROJECT_STEPS - 1)
    def _():
        for h in range(HEADS):
            g = h // SHARE
            out_ref[h, 0:STATE, :] = acc_ref[g * STATE : (g + 1) * STATE]
            out_ref[h, STATE : 2 * STATE, :] = acc_ref[128 + g * STATE : 128 + (g + 1) * STATE]
            out_ref[h, 2 * STATE :, :] = jnp.broadcast_to(
                acc_ref[256 + h : 257 + h], (COLS - 2 * STATE, ROWS)
            )


def project(core, hidden, own, other):
    _, width, half = own.shape
    many = PARTS // PROJECT_STEPS
    return pl.pallas_call(
        project_kernel,
        out_shape=jax.ShapeDtypeStruct((HEADS, COLS, ROWS), F32),
        grid_spec=pltpu.PrefetchScalarGridSpec(
            num_scalar_prefetch=1,
            grid=(PROJECT_STEPS,),
            in_specs=[
                pl.BlockSpec((1, ROWS, many * 2 * half), lambda i, c: (0, 0, i)),
                pl.BlockSpec((many, width, half), lambda i, c: (i, 0, 0)),
                pl.BlockSpec((many, width, half), lambda i, c: (i, 0, 0)),
            ],
            out_specs=pl.BlockSpec((HEADS, COLS, ROWS), lambda i, c: (0, 0, 0)),
            scratch_shapes=[pltpu.VMEM((width, ROWS), F32)],
        ),
        compiler_params=params(24),
        cost_estimate=pl.CostEstimate(
            flops=2 * ROWS * D * 288, bytes_accessed=8 << 20, transcendentals=0
        ),
    )(core, hidden, own, other)


def attend_kernel(
    core_ref,
    own_ref,
    other_ref,
    teach_ref,
    v_ref,
    vt_ref,
    n_ref,
    queries,
    labels,
    keys,
    values,
    turned,
    mixed,
    scores,
    sems,
    out_sems,
):
    first = PAD // ROWS
    key_part = keys.at[pl.ds(first, BLOCKS)]
    docs_in = pltpu.make_async_copy(own_ref.at[:, pl.ds(2 * ROWS, DOC_ROWS)], labels, sems.at[0])
    query_in = pltpu.make_async_copy(own_ref.at[:, pl.ds(0, ROWS)], queries, sems.at[1])
    own_kv = own_ref.at[:, pl.ds(ROWS, ROWS)]
    is_key = core_ref[0] == 0

    @pl.when(is_key)
    def _():
        pltpu.make_async_copy(other_ref, values, sems.at[2]).start()
        pltpu.make_async_copy(own_kv, key_part, sems.at[3]).start()

    @pl.when(jnp.logical_not(is_key))
    def _():
        pltpu.make_async_copy(own_kv, values, sems.at[2]).start()
        pltpu.make_async_copy(other_ref, key_part, sems.at[3]).start()

    docs_in.start()
    query_in.start()
    keys[0:first] = jnp.zeros((first, ROWS, DIM), BF16)
    turned[:, 0:PAD] = jnp.zeros((DIM, PAD), BF16)
    pltpu.make_async_copy(other_ref, values, sems.at[2]).wait()
    v_out = pltpu.make_async_copy(values, v_ref, out_sems.at[0])
    v_out.start()
    for s in range(BLOCKS):
        turned[:, PAD + s * ROWS : PAD + (s + 1) * ROWS] = values[s].T
    vt_out = pltpu.make_async_copy(turned.at[:, pl.ds(PAD, SEQ)], vt_ref, out_sems.at[1])
    vt_out.start()
    docs_in.wait()
    docs = jnp.max(labels[...].astype(F32), axis=1)
    for d in range(3):
        n_ref[d] = jnp.sum((docs < d + 0.5).astype(F32)).astype(jnp.int32)
    n_ref[3] = 0
    query_in.wait()
    pltpu.make_async_copy(other_ref, key_part, sems.at[3]).wait()

    scale = DIM ** (-0.5) * math.log2(math.e)

    def rows(i, carry):
        q0 = i * QUERIES
        many = QUERIES // ROWS
        query = queries[pl.ds(many * i, many)].reshape(QUERIES, DIM)
        first = scalar_start(q0, n_ref)
        need = q0 + QUERIES - first
        rest = lax.rem(need, KEYS)
        count = need // KEYS + (rest > HALF).astype(jnp.int32)
        ends = ((rest > 0) & (rest <= HALF)).astype(jnp.int32)
        q_at = q0 + lax.broadcasted_iota(jnp.int32, (1, QUERIES), 1)
        start = doc_start(q_at, n_ref)

        def tile(at, size):
            low = q0 + QUERIES - at - size
            return low, low + PAD, pl.ds(pl.multiple_of(at, HALF), size)

        def score(at, size, top):
            low, key_at, rows_at = tile(at, size)
            block = keys[pl.ds(key_at // ROWS, size // ROWS)].reshape(size, DIM)
            s = mm_nt(block, query)
            k_at = low + lax.broadcasted_iota(jnp.int32, (size, QUERIES), 0)
            s = jnp.where((k_at <= q_at) & (k_at >= start), s, NEG)
            scores[rows_at, :] = s
            return jnp.maximum(top, jnp.max(s.reshape(size // 8, 8, QUERIES), axis=0))

        def masked(j, top):
            return score(j * KEYS, KEYS, top)

        def masked_half(j, top):
            return score(count * KEYS, HALF, top)

        top = jnp.full((8, QUERIES), NEG, F32)
        top = lax.fori_loop(0, count, masked, top)
        top = lax.fori_loop(0, ends, masked_half, top)
        top = jnp.max(top, axis=0, keepdims=True)

        def mix(at, size, state):
            total, out = state
            _, key_at, rows_at = tile(at, size)
            p = jnp.exp2((scores[rows_at, :] - top) * scale)
            total = total + jnp.sum(p.reshape(size // 8, 8, QUERIES), axis=0)
            return total, out + mm(
                turned[:, pl.ds(pl.multiple_of(key_at, HALF), size)], p.astype(BF16)
            )

        state = (jnp.zeros((8, QUERIES), F32), jnp.zeros((DIM, QUERIES), F32))
        state = lax.fori_loop(0, count, lambda j, t: mix(j * KEYS, KEYS, t), state)
        total, out = lax.fori_loop(0, ends, lambda j, t: mix(count * KEYS, HALF, t), state)
        total = jnp.sum(total, axis=0, keepdims=True)
        mixed[i] = (out / total).astype(BF16)
        teach_out(i).start()
        return carry

    def teach_out(i):
        lanes = pl.ds(pl.multiple_of(i * QUERIES, QUERIES), QUERIES)
        return pltpu.make_async_copy(mixed.at[i], teach_ref.at[:, lanes], out_sems.at[2 + i])

    lax.fori_loop(0, SEQ // QUERIES, rows, 0)
    v_out.wait()
    vt_out.wait()
    for i in range(SEQ // QUERIES):
        teach_out(i).wait()


def attend(core, own, other):
    many = SEQ // QUERIES
    return pl.pallas_call(
        attend_kernel,
        out_shape=(
            jax.ShapeDtypeStruct((DIM, SEQ), BF16),
            jax.ShapeDtypeStruct((BLOCKS, ROWS, DIM), BF16),
            jax.ShapeDtypeStruct((DIM, SEQ), BF16),
            jax.ShapeDtypeStruct((4,), jnp.int32),
        ),
        in_specs=[SMEM, ANY, ANY],
        out_specs=(ANY, ANY, ANY, SMEM),
        scratch_shapes=[
            pltpu.VMEM((BLOCKS, ROWS, DIM), BF16),
            pltpu.VMEM((BLOCKS, DOC_ROWS, DIM), BF16),
            pltpu.VMEM((BLOCKS + PAD // ROWS, ROWS, DIM), BF16),
            pltpu.VMEM((BLOCKS, ROWS, DIM), BF16),
            pltpu.VMEM((DIM, PAD + SEQ), BF16),
            pltpu.VMEM((many, DIM, QUERIES), BF16),
            pltpu.VMEM((SEQ + KEYS, QUERIES), F32),
            pltpu.SemaphoreType.DMA((4,)),
            pltpu.SemaphoreType.DMA((2 + many,)),
        ],
        compiler_params=params(),
        cost_estimate=pl.CostEstimate(
            flops=8 << 30, bytes_accessed=8 << 20, transcendentals=8 << 20
        ),
    )(core, own, other)


def scan_lanes(x, reverse):
    width = x.shape[1]
    lane = lax.broadcasted_iota(jnp.int32, x.shape, 1)
    step = 1
    while step < width:
        if reverse:
            moved = pltpu.roll(x, width - step, 1)
            x = x + jnp.where(lane < width - step, moved, 0.0)
        else:
            moved = pltpu.roll(x, step, 1)
            x = x + jnp.where(lane >= step, moved, 0.0)
        step *= 2
    return x


def student_kernel(
    head_ref,
    n_ref,
    bias_ref,
    rate_ref,
    taps_ref,
    proj_ref,
    teach_ref,
    v_ref,
    vt_ref,
    out_ref,
    source,
    steps,
    cums,
    columns,
    pre_s,
    sig_s,
    z_s,
    dc_s,
    q_s,
    x_s,
    direct_s,
    state_s,
    dstate_s,
    *,
    weight,
):
    head = head_ref[0]
    group = head // SHARE
    bias = bias_ref[head]
    rate = rate_ref[head]
    lane = lax.broadcasted_iota(jnp.int32, (1, SPAN), 1)
    deep = lax.broadcasted_iota(jnp.int32, (SPAN, SPAN), 0)
    taps_b = taps_ref[pl.ds(pl.multiple_of(group * STATE, STATE), STATE), :]
    taps_c = taps_ref[pl.ds(pl.multiple_of(128 + group * STATE, STATE), STATE), :]
    taps = jnp.concatenate([taps_b, taps_c], 0)

    source[:, 0:128] = jnp.zeros((2 * STATE, 128), F32)
    for s in range(BLOCKS):
        source[:, 128 + s * ROWS : 128 + (s + 1) * ROWS] = proj_ref[s, 0 : 2 * STATE, :]
        steps[s // 2 : s // 2 + 1, (s % 2) * ROWS : (s % 2 + 1) * ROWS] = proj_ref[
            s, 2 * STATE : 2 * STATE + 1, :
        ]
    raw = steps[...] + bias
    step_all = jnp.maximum(raw, 0.0) + jnp.log1p(jnp.exp(-jnp.abs(raw)))
    slope_all = 1.0 / (1.0 + jnp.exp(-raw))
    steps[...] = step_all
    cum_all = scan_lanes(-step_all * rate, False)
    cums[...] = cum_all
    cum_turned = cum_all.T
    for c in range(CHUNKS):
        columns[c] = cum_turned[:, c : c + 1]

    def marks(c):
        base = c * SPAN
        at = base + lane
        start = doc_start(at, n_ref)
        last = scalar_start(base + SPAN - 1, n_ref)
        return base, at, start, last

    def forward(c, state):
        base, at, start, last = marks(c)
        wide = pl.multiple_of(base, SPAN)
        rows = source[:, pl.ds(wide, SPAN + 128)]
        pre = taps[:, 0:1] * rows[:, 128:]
        for j in range(1, TAPS):
            lagged = jnp.where(at - j >= start, pltpu.roll(rows, j, 1)[:, 128:], 0.0)
            pre = pre + taps[:, j : j + 1] * lagged
        sig = 1.0 / (1.0 + jnp.exp(-pre))
        gates = pre * sig
        pre_s[:, pl.ds(wide, SPAN)] = pre
        sig_s[:, pl.ds(wide, SPAN)] = sig
        gate_c = gates[STATE:]
        step = steps[pl.ds(c, 1), :]
        cum = cums[pl.ds(c, 1), :]
        ended = cum[:, SPAN - 1 :]
        fed = gates[:STATE] * step
        fed_high, fed_low = split(fed)
        c_high, c_low = split(gate_c)
        fed_stack = jnp.concatenate([fed, fed_low.astype(F32), fed], 0)
        left = fed_stack.T.astype(BF16)
        inner = mm(left, jnp.concatenate([c_high, c_high, c_low], 0))
        allowed = (deep <= lane) & (deep >= start - base)
        fade = jnp.exp(jnp.where(allowed, cum - columns[c], NEG))
        mixing = fade * inner
        mix_high, mix_low = split(mixing)
        values = v_ref[pl.ds(2 * c, 2)].reshape(SPAN, DIM)
        turned = vt_ref[:, pl.ds(wide, SPAN)]
        enter = jnp.where(start < base, jnp.exp(cum), 0.0)
        entered = gate_c * enter
        in_high, in_low = split(entered)
        s_high, s_low = split(state)
        state_left = jnp.concatenate([state, s_low.astype(F32), state], 0).T.astype(BF16)
        out = mm(turned, mix_high) + mm(turned, mix_low)
        out = out + mm(state_left, jnp.concatenate([in_high, in_high, in_low], 0))
        wanted = teach_ref[:, pl.ds(wide, SPAN)].astype(F32)
        error = (out - wanted) * weight
        q_s[pl.ds(c, 1), :] = jnp.sum(out * error, axis=0, keepdims=True)
        e_high, e_low = split(error)
        e_stack = jnp.concatenate([e_high, e_low], 0)
        pulled = fade * mm(jnp.concatenate([values, values], 1), e_stack)
        h_high, h_low = split(pulled)
        c_stack = jnp.concatenate([c_high, c_low], 0)
        z = mm_nt(c_stack, h_high) + mm_nt(c_stack, h_low)
        z_s[:, pl.ds(wide, SPAN)] = z[:STATE] + z[STATE:]
        fed_pair = jnp.concatenate([fed_high, fed_low], 0)
        dc = mm(fed_pair, h_high) + mm(fed_pair, h_low)
        s_pair = jnp.concatenate([s_high, s_low], 0)
        dc_in = mm(s_pair, e_high) + mm(s_pair, e_low)
        dc_s[:, pl.ds(wide, SPAN)] = dc[:STATE] + dc[STATE:] + enter * (dc_in[:STATE] + dc_in[STATE:])
        in_pair = jnp.concatenate([in_high, in_low], 0)
        ds = mm_nt(in_pair, e_high) + mm_nt(in_pair, e_low)
        dstate_s[c] = ds[:STATE] + ds[STATE:]
        state_s[c] = state
        tail = jnp.where(at >= last, jnp.exp(ended - cum), 0.0)
        t_high, t_low = split(fed * tail)
        new = mm(jnp.concatenate([t_high, t_low], 0), values)
        keep = jnp.where(last < base, 1.0, 0.0) * jnp.exp(ended)
        return keep * state + new[:STATE] + new[STATE:]

    final = lax.fori_loop(0, CHUNKS, forward, jnp.zeros((STATE, DIM), F32), unroll=UNROLL)
    state_s[CHUNKS] = final

    def backward(k, carried):
        dstate, later = carried
        c = CHUNKS - 1 - k
        base, at, start, last = marks(c)
        wide = pl.multiple_of(base, SPAN)
        step = steps[pl.ds(c, 1), :]
        cum = cums[pl.ds(c, 1), :]
        ended = cum[:, SPAN - 1 :]
        tail = jnp.where(at >= last, jnp.exp(ended - cum), 0.0)
        d_high, d_low = split(dstate)
        turned = vt_ref[:, pl.ds(wide, SPAN)]
        through = mm(jnp.concatenate([d_high, d_low], 0), turned)
        z = z_s[:, pl.ds(wide, SPAN)] + tail * (through[:STATE] + through[STATE:])
        pre = pre_s[:, pl.ds(wide, SPAN)]
        sig = sig_s[:, pl.ds(wide, SPAN)]
        gates = pre * sig
        direct = jnp.sum(gates[:STATE] * z, axis=0, keepdims=True)
        direct_s[pl.ds(c, 1), :] = direct
        crossing = jnp.sum(jnp.sum(dstate * state_s[c + 1], axis=0, keepdims=True), axis=1, keepdims=True)
        x_s[pl.ds(c, 1), :] = jnp.broadcast_to(crossing, (1, SPAN))
        dgates = jnp.concatenate([step * z, dc_s[:, pl.ds(wide, SPAN)]], 0)
        dpre = dgates * (sig + gates * (1.0 - sig))
        rows = jnp.concatenate([dpre, later], 1)
        back = taps[:, 0:1] * rows[:, :SPAN]
        for j in range(1, TAPS):
            reach = jnp.where(at >= doc_start(at + j, n_ref), pltpu.roll(rows, SPAN + 128 - j, 1)[:, :SPAN], 0.0)
            back = back + taps[:, j : j + 1] * reach
        out_ref[2 * c, 0 : 2 * STATE, :] = back[:, :ROWS]
        out_ref[2 * c + 1, 0 : 2 * STATE, :] = back[:, ROWS:]
        keep = jnp.where(last < base, 1.0, 0.0) * jnp.exp(ended)
        return keep * dstate + dstate_s[c], dpre[:, :128]

    nothing = (jnp.zeros((STATE, DIM), F32), jnp.zeros((2 * STATE, 128), F32))
    lax.fori_loop(0, CHUNKS, backward, nothing, unroll=UNROLL)

    at_all = lax.broadcasted_iota(jnp.int32, (CHUNKS, SPAN), 0) * SPAN
    at_all = at_all + lax.broadcasted_iota(jnp.int32, (CHUNKS, SPAN), 1)
    direct = direct_s[...]
    dlog = scan_lanes(q_s[...] - step_all * direct, True) + x_s[...]
    dlog = jnp.where(at_all > doc_start(at_all, n_ref), dlog, 0.0)
    dstep = (direct - rate * dlog) * slope_all
    for s in range(BLOCKS):
        piece = dstep[s // 2 : s // 2 + 1, (s % 2) * ROWS : (s % 2 + 1) * ROWS]
        out_ref[s, 2 * STATE :, :] = jnp.broadcast_to(piece, (COLS - 2 * STATE, ROWS))


def student(head, counts, bias, rate, taps, proj, teach, v, vt, weight):
    return pl.pallas_call(
        lambda *refs: student_kernel(*refs, weight=weight),
        out_shape=jax.ShapeDtypeStruct((BLOCKS, COLS, ROWS), F32),
        in_specs=[SMEM, SMEM, SMEM, SMEM, VMEM, VMEM, VMEM, VMEM, VMEM],
        out_specs=VMEM,
        scratch_shapes=[
            pltpu.VMEM((2 * STATE, 128 + SEQ), F32),
            pltpu.VMEM((CHUNKS, SPAN), F32),
            pltpu.VMEM((CHUNKS, SPAN), F32),
            pltpu.VMEM((CHUNKS, SPAN, 1), F32),
            pltpu.VMEM((2 * STATE, SEQ), F32),
            pltpu.VMEM((2 * STATE, SEQ), F32),
            pltpu.VMEM((STATE, SEQ), F32),
            pltpu.VMEM((STATE, SEQ), F32),
            pltpu.VMEM((CHUNKS, SPAN), F32),
            pltpu.VMEM((CHUNKS, SPAN), F32),
            pltpu.VMEM((CHUNKS, SPAN), F32),
            pltpu.VMEM((CHUNKS + 1, STATE, DIM), F32),
            pltpu.VMEM((CHUNKS, STATE, DIM), F32),
        ],
        compiler_params=params(56),
        cost_estimate=pl.CostEstimate(
            flops=8 << 30, bytes_accessed=8 << 20, transcendentals=4 << 20
        ),
    )(head, counts, bias, rate, taps, proj, teach, v, vt)


def combine_kernel(in_ref, out_ref, rows):
    for g in range(GROUPS):
        gates = in_ref[SHARE * g, : 2 * STATE]
        for k in range(1, SHARE):
            gates = gates + in_ref[SHARE * g + k, : 2 * STATE]
        rows[g * STATE : (g + 1) * STATE] = gates[:STATE]
        rows[128 + g * STATE : 128 + (g + 1) * STATE] = gates[STATE:]
    for h in range(HEADS):
        rows[256 + h : 257 + h] = in_ref[h, 2 * STATE : 2 * STATE + 1]
    out_ref[...] = rows[...].astype(BF16)


def combine(parts):
    return pl.pallas_call(
        combine_kernel,
        out_shape=jax.ShapeDtypeStruct((WIDTH, ROWS), BF16),
        in_specs=[VMEM],
        out_specs=VMEM,
        scratch_shapes=[pltpu.VMEM((WIDTH, ROWS), F32)],
        compiler_params=params(16),
    )(parts)


def product_kernel(core_ref, *refs):
    count = PARTS // 2 + 1
    grads, blocks, (keep_ref, send_ref) = refs[:count], refs[count : 2 * count], refs[2 * count :]
    left = []
    for grad in grads:
        left += [grad[...]] if len(grad.shape) == 2 else [grad[0], grad[1]]
    left = jnp.concatenate(left, 1)
    half = blocks[0].shape[-1] // 2
    for ref, core in ((send_ref, 1 - core_ref[0]), (keep_ref, core_ref[0])):
        lanes = pl.ds(pl.multiple_of(core * half, half), half)
        right = []
        for block in blocks:
            if len(block.shape) == 2:
                right.append(block[:, lanes])
            else:
                right += [block[0, :, lanes], block[1, :, lanes]]
        part = mm(left, jnp.concatenate(right, 0))
        for r in range(4):
            for q in range(4):
                ref[4 * r + q] = part[r * 72 : (r + 1) * 72, q * 128 : (q + 1) * 128]


def product(core, grads, blocks):
    shape = jax.ShapeDtypeStruct((16, WIDTH // 4, 128), F32)
    return pl.pallas_call(
        product_kernel,
        out_shape=(shape, shape),
        in_specs=[SMEM] + [VMEM] * (PARTS + 2),
        out_specs=(VMEM, VMEM),
        compiler_params=params(24),
        cost_estimate=pl.CostEstimate(
            flops=2 * WIDTH * 1024 * 1024, bytes_accessed=4 << 20, transcendentals=0
        ),
    )(core, *grads, *blocks)


def arrange_kernel(core_ref, own_ref, other_ref, out_ref):
    half = out_ref.shape[1] // 2
    for ref, core in ((own_ref, core_ref[0]), (other_ref, 1 - core_ref[0])):
        for r in range(4):
            for q in range(4):
                lanes = pl.ds(pl.multiple_of(core * half + q * 128, 128), 128)
                out_ref[r * 72 : (r + 1) * 72, lanes] = ref[4 * r + q]


def arrange(core, own, other):
    return pl.pallas_call(
        arrange_kernel,
        out_shape=jax.ShapeDtypeStruct((WIDTH, D // PARTS), F32),
        in_specs=[SMEM, VMEM, VMEM],
        out_specs=VMEM,
        compiler_params=params(16),
    )(core, own, other)


def swap_all(x, axis, groups=None):
    return lax.all_to_all(x, axis, 0, 0, tiled=True, axis_index_groups=groups)


def both_ways(block, distance):
    route = []
    for s in range(lax.axis_size("seq")):
        sign = 1 - 2 * (s % 2)
        for z in range(PARTS):
            route.append((s * PARTS + z, s * PARTS + (z + sign * distance) % PARTS))
    return lax.ppermute(block, ("seq", "dp"), route)


def local(hidden, queries, keys, values, docs, w_proj, conv_weight, dt_bias, decay_rate):
    seq_devices = lax.axis_size("seq")
    data_devices = lax.axis_size("dp")
    seq_len = hidden.shape[1] * seq_devices
    weight = 1.0 / math.sqrt(HEADS * DIM * data_devices * seq_len)
    head = lax.axis_index("seq").astype(jnp.int32)
    core = lax.rem(head, 2)[None]
    part = lax.axis_index("dp").astype(jnp.int32)[None]
    same_core = [[2 * i + c for i in range(seq_devices // 2)] for c in range(2)]
    partner = [(i, i ^ 1) for i in range(seq_devices)]

    turned_w = w_proj.T
    half = turned_w.shape[1] // 2
    own_w = lax.dynamic_slice_in_dim(turned_w, core[0] * half, half, 1)
    own_w = lax.all_gather(own_w, "dp", axis=0)
    own = swap_all(pack_teacher(queries, keys, values, docs), "seq")
    stay, across, mine, give = pack_hidden(core, part, hidden)
    taken = lax.ppermute(give, "seq", partner)
    outgoing = [across] + [jnp.stack([mine[k], taken[k]]) for k in range(PARTS // 2 - 1)]
    own, outgoing, taps = lax.optimization_barrier((own, outgoing, conv_weight.T))
    shared = own[:, ROWS : 2 * ROWS, :]
    own, shared, own_w, outgoing = lax.optimization_barrier((own, shared, own_w, outgoing))
    other_w = lax.ppermute(own_w, "seq", partner)
    other = lax.ppermute(shared, "seq", partner)
    far = PARTS // 2
    arrived = {far: both_ways(outgoing[0], far)}
    for k in (3, 2):
        arrived[k] = both_ways(outgoing[k], k)
    late = {k: outgoing[k] for k in (1,)}
    proj = swap_all(project(core, hidden, own_w, other_w), "seq")
    teach, v, vt, counts = attend(core, own, other)
    grads = student(
        head[None], counts, dt_bias, decay_rate, taps, proj, teach, v, vt, weight
    )
    grads, arrived, late = lax.optimization_barrier((grads, arrived, late))
    late = {k: both_ways(late[k], k) for k in late}
    rounded, late = lax.optimization_barrier((combine(swap_all(grads, "seq")), late))
    arrived.update(late)
    spread_grads = {far: both_ways(rounded, far)}
    pair = jnp.stack([rounded, lax.ppermute(rounded, "seq", partner)])
    order = (far, 3, 2, 1)
    for k in order[1:]:
        spread_grads[k] = both_ways(pair, k)
    keep, send = product(
        core,
        [rounded] + [spread_grads[k] for k in order],
        [stay] + [arrived[k] for k in order],
    )
    partial = keep + lax.ppermute(send, "seq", partner)
    total = jnp.sum(swap_all(partial, "seq", same_core), axis=0)
    spread = jnp.broadcast_to(total[None], partial.shape)
    own_blocks = swap_all(spread, "seq", same_core)
    other_blocks = lax.ppermute(own_blocks, "seq", partner)
    return arrange(core, own_blocks, other_blocks).T


def solution(mesh):
    placed = (
        P("dp", "seq", None),
        P("dp", "seq", None),
        P("dp", "seq", None),
        P("dp", "seq", None),
        P("dp", "seq"),
        P("dp", None),
        P(),
        P(),
        P(),
    )
    return jax.shard_map(
        local, mesh=mesh, in_specs=placed, out_specs=P("dp", None), check_vma=False
    )
```
